512 devices in a mesh: row: 64 (over y, z_hi, core), col: 8 (over z_lo, x).
Axes of the slice: x: 4, y: 8, z: 8 (z_hi: 4, z_lo: 2; z = z_hi * 2 + z_lo), core: 2. Of those that a mesh axis runs over, the one named last changes fastest.
Arguments:
- grad_out: bfloat16 [256, 32768], P('col', 'row'), may hold values from -0.15917969 to 0.15917969
- pre_act: bfloat16 [256, 32768], P('col', 'row'), may hold values from -6 to 6
- aggregated: bfloat16 [256, 32768], P('col', 'row'), may hold values from -6 to 6
- weight: bfloat16 [256, 256], P(None, 'col'), may hold values from -0.375 to 0.375
- tiles: bfloat16 [6336, 128, 128], P('row'), may hold values from -6 to 6
- tile_coords: int32 [6336, 2], P('row'), may hold values from 0 to 255, as said below
- tile_count: int32 [64], P('row'), may hold values from 8 to 99
Outputs:
- feature_grad: bfloat16 [256, 32768], P('col', 'row')
- weight_grad: float32 [256, 256], P('col')
The draws below stay inside these ranges and needn't reach their ends.
Inputs may be any that keep to these rules, and one draw needn't show every extreme that they name: `tile_coords`: the block column of every slot of node block b lies within b's own node block (b * 4 to b * 4 + 3). The slots in use are ordered by the node block holding their block row, rising; at most 8 slots in use of one node block have their block rows in one node block, and that many is reached. Slots beyond tile_count hold arbitrary coordinates within the range.
All inputs are finite; a program needn't handle non-finite values.
Results may differ from the reference program's by a relative error of at most 0.011.
Values may be sent and summed in bfloat16 or wider, within the bound.
A program may use at most 64 MiB of HBM per device.

```python
import jax
import jax.numpy as jnp
from jax import lax

F = 256
TILE = 128
MAXS = 8
BLOCKS_DEV = 4
MAXT = 99
NODES = 32768
N_ROW = 64


def tile_plan(key):
    loop_size = N_ROW
    keys = jax.random.split(key, 5)
    dev_ids = jnp.arange(loop_size, dtype=jnp.int32)[:, None]
    src_ids = jnp.arange(loop_size, dtype=jnp.int32)[None, :]
    offset = (src_ids - dev_ids) % loop_size
    distance = jnp.minimum(offset, loop_size - offset)
    near_counts = jax.random.randint(keys[0], (loop_size, loop_size), 0, MAXS + 1)
    far_counts = jax.random.randint(keys[1], (loop_size, loop_size), 0, 2)
    full_device = jax.random.randint(keys[2], (), 0, loop_size)
    counts = jnp.where(distance == 0, MAXS, jnp.where(distance <= 2, near_counts, far_counts))
    full_row = jnp.where(distance == 0, MAXS, jnp.where(distance <= 2, MAXS, 1))
    counts = jnp.where(dev_ids == full_device, full_row, counts).astype(jnp.int32)
    running = jnp.cumsum(counts, axis=1)
    slot_ids = jnp.arange(MAXT, dtype=jnp.int32)
    source = jnp.sum((running[:, None, :] <= slot_ids[None, :, None]).astype(jnp.int32), axis=2)
    source = jnp.minimum(source, loop_size - 1)
    block_row = source * BLOCKS_DEV + jax.random.randint(keys[3], (loop_size, MAXT), 0, BLOCKS_DEV)
    block_col = dev_ids * BLOCKS_DEV + jax.random.randint(keys[4], (loop_size, MAXT), 0, BLOCKS_DEV)
    coords = jnp.stack([block_row, block_col], axis=-1).reshape(loop_size * MAXT, 2).astype(jnp.int32)
    return (coords, running[:, -1].astype(jnp.int32))


def draw_tile_coords(key, part):
    return tile_plan(key)[0]


def draw_tile_count(key, part):
    return tile_plan(key)[1]


def level_of(own_key, dims, cuts, least, top_value):
    factor_of, own = 1.0, jax.random.fold_in(own_key, 6)
    for position, shards_of in cuts:
        steps = jnp.exp(jax.random.uniform(jax.random.fold_in(own, position), (shards_of,), jnp.float32, least / len(cuts), top_value / len(cuts)))
        factor_of = factor_of * jnp.repeat(steps, dims[position] // shards_of).reshape([-1 if axis == position else 1 for axis in range(len(dims))])
    return factor_of


def centred(stream_key, dims, width, most, pieces=(), held_as=jnp.bfloat16):
    entries = width * jax.random.normal(stream_key, dims, jnp.float32)
    if pieces:
        entries = entries * level_of(stream_key, dims, pieces, -0.22, 0.18)
    return jnp.clip(entries, -most, most).astype(held_as)


def setup_inputs(seed: int = 0) -> dict:
    streams_of = jax.random.split(jax.random.key(seed), 8)
    grad_out = centred(streams_of[0], (F, NODES), 0.02, 0.15917969, ((0, 8), (1, 64)))
    pre_act = centred(streams_of[1], (F, NODES), 1.0, 6.0, ((0, 8), (1, 64)))
    aggregated = centred(streams_of[2], (F, NODES), 1.0, 6.0, ((0, 8), (1, 64)))
    weight = centred(streams_of[3], (F, F), F ** -0.5, 0.375, ((1, 8),))
    tiles = centred(streams_of[4], (MAXT * N_ROW, TILE, TILE), 1.0, 6.0, ((0, 64),))
    tile_coords = draw_tile_coords(jax.random.fold_in(streams_of[7], 71), 0)
    tile_count = draw_tile_count(jax.random.fold_in(streams_of[7], 71), 0)
    return dict(grad_out=grad_out, pre_act=pre_act, aggregated=aggregated, weight=weight, tiles=tiles, tile_coords=tile_coords, tile_count=tile_count)


def reference(grad_out, pre_act, aggregated, weight, tiles, tile_coords, tile_count):
    masked = jnp.where(pre_act > 0, grad_out, jnp.zeros_like(grad_out))
    node_grad = jnp.dot(weight, masked, preferred_element_type=jnp.float32).astype(jnp.bfloat16)
    weight_grad = lax.dot_general(aggregated, masked, (((1,), (1,)), ((), ())), preferred_element_type=jnp.float32)
    blocks = node_grad.reshape(F, NODES // TILE, TILE)
    tiles_r = tiles.reshape(N_ROW, MAXT, TILE, TILE)
    coords_r = tile_coords.reshape(N_ROW, MAXT, 2)

    def per_device(packed):
        dev_tiles, dev_coords, dev_count, dev_index = packed
        block_piece = jnp.take(blocks, dev_coords[:, 0], axis=1).astype(jnp.float32)
        products = jnp.einsum('fmi,mij->fmj', block_piece, dev_tiles.astype(jnp.float32))
        in_use = jnp.arange(MAXT, dtype=jnp.int32) < dev_count
        local_col = dev_coords[:, 1] - dev_index * BLOCKS_DEV
        col_onehot = ((local_col[:, None] == jnp.arange(BLOCKS_DEV, dtype=jnp.int32)[None, :]) & in_use[:, None]).astype(jnp.float32)
        return jnp.einsum('fmj,mb->fbj', products, col_onehot)

    per_dev_out = lax.map(per_device, (tiles_r, coords_r, tile_count, jnp.arange(N_ROW, dtype=jnp.int32)))
    feature_grad = per_dev_out.transpose(1, 0, 2, 3).reshape(F, NODES).astype(jnp.bfloat16)
    return feature_grad, weight_grad
```

```python
import jax
import jax.numpy as jnp
from jax import lax
from jax.experimental import pallas as pl
from jax.experimental.pallas import tpu as pltpu
from jax.sharding import PartitionSpec as P

YN, ZN, CORES, COLS = 8, 4, 2, 8
WN = ZN * CORES
ROWS = YN * WN
TILE = 128
BLOCKS = 4
FEAT = 32
NODES = BLOCKS * TILE
SLOTS = 99
MESH = pl.DeviceIdType.MESH
ZORDER = (0, 1, 3, 2)


def kernel(
    go_hbm, pa_hbm, agg_hbm, wt_hbm, tiles_hbm, coords_hbm, count_hbm,
    fg_out, wg_out,
    go, pa, agg, wt, tiles, coords, count,
    masked, wpart, wrow, x, wl, ra, part, rb, final,
    in_sem, m_send, m_recv, w_send, w_recv, z_send, z_recv,
    y_send, y_recv, s_send, s_recv, a_send, a_recv, b_send, b_recv, c_send, c_recv,
):
    row = lax.axis_index("row")
    col = lax.axis_index("col")
    y = row // WN
    w = row % WN
    z = w // CORES
    core = w % CORES
    sibling = row + 1 - 2 * core

    def at_col(o):
        return {"row": row, "col": (col + o) % COLS}

    def at_row(r):
        return {"row": r, "col": col}

    def y_row(o):
        return ((y + o) % YN) * WN + w

    def w_row(o):
        return y * WN + (w + o) % WN

    def z_row(o):
        return y * WN + ((z + o) % ZN) * CORES + core

    barrier = pltpu.get_barrier_semaphore()
    for o in range(1, COLS):
        pl.semaphore_signal(barrier, inc=1, device_id=at_col(o), device_id_type=MESH)
    for o in range(1, YN):
        pl.semaphore_signal(barrier, inc=1, device_id=at_row(y_row(o)), device_id_type=MESH)
    for o in range(1, WN):
        pl.semaphore_signal(barrier, inc=1, device_id=at_row(w_row(o)), device_id_type=MESH)

    loads = [
        pltpu.make_async_copy(src, dst, in_sem.at[n])
        for n, (src, dst) in enumerate((
            (go_hbm, go), (pa_hbm, pa), (wt_hbm, wt), (agg_hbm, agg),
            (coords_hbm, coords), (count_hbm, count), (tiles_hbm, tiles),
        ))
    ]
    for load in loads:
        load.start()
    loads[0].wait()
    loads[1].wait()
    masked[col] = jnp.where(pa[...] > 0, go[...], jnp.zeros_like(go[...]))
    loads[2].wait()
    wpart[col] = wt[:, pl.ds(pl.multiple_of((col // 4) * TILE, TILE), TILE)]

    pl.semaphore_wait(barrier, COLS - 1 + YN - 1 + WN - 1)

    def remote(src, dst, send, recv, to):
        return pltpu.make_async_remote_copy(
            src_ref=src, dst_ref=dst, send_sem=send, recv_sem=recv,
            device_id=to, device_id_type=MESH,
        )

    sends = []

    def send(src, dst, send_sem, recv_sem, to):
        copy = remote(src, dst, send_sem, recv_sem, to)
        copy.start()
        sends.append(copy)

    for o in range(1, COLS):
        peer = (col + o) % COLS
        send(
            wt.at[:, pl.ds(pl.multiple_of((peer // 4) * TILE, TILE), TILE)],
            wpart.at[col], w_send.at[o], w_recv.at[COLS - o], at_col(o),
        )
        send(masked.at[col], masked.at[col], m_send.at[o], m_recv.at[COLS - o], at_col(o))
    for o in range(1, COLS):
        peer = (col + o) % COLS
        remote(wpart.at[peer], wpart.at[peer], w_send.at[o], w_recv.at[o], at_col(o)).wait_recv()
    wrow[...] = wpart[...].reshape(COLS * FEAT, TILE).astype(jnp.float32).T
    own_w = wrow[pl.ds(pl.multiple_of((col % 4) * FEAT, FEAT), FEAT), :].astype(jnp.bfloat16)
    for o in range(1, COLS):
        peer = (col + o) % COLS
        remote(masked.at[peer], masked.at[peer], m_send.at[o], m_recv.at[o], at_col(o)).wait_recv()

    m_all = masked[...].reshape(COLS * FEAT, NODES)
    node_grad = jnp.dot(own_w, m_all, preferred_element_type=jnp.float32).astype(jnp.bfloat16)
    for b in range(BLOCKS):
        x[row * BLOCKS + b] = node_grad[:, b * TILE:(b + 1) * TILE]

    def block(r):
        return x.at[pl.ds(r * BLOCKS, BLOCKS)]

    def to_y(step, d, k, r):
        send(block(r), block(r), y_send.at[step, k, d], y_recv.at[step, k + 1, d],
             at_row(y_row(1 - 2 * step)))

    def to_sibling(step, d, k, r):
        send(block(r), block(r), s_send.at[step, k, d], s_recv.at[step, k, d], at_row(sibling))

    def source(step, d, k):
        return ((y - (1 - 2 * step) * k) % YN) * WN + ((z + d) % ZN) * CORES + core

    own = block(row)
    to_y(0, 0, 0, row)
    to_y(1, 0, 0, row)
    for d in (1, 3, 2):
        send(own, own, z_send.at[d], z_recv.at[ZN - d], at_row(z_row(d)))
    to_sibling(0, 0, 0, row)

    loads[3].wait()
    wgrad = lax.dot_general(
        agg[...], m_all, (((1,), (1,)), ((), ())), preferred_element_type=jnp.float32
    )
    for q in range(YN):
        piece = wgrad[(q // 2) * 8:(q // 2) * 8 + 8, (q % 2) * TILE:(q % 2 + 1) * TILE]
        wl[q] = piece
    ra[y] = wl[y]
    for o in range(1, YN):
        send(wl.at[(y + o) % YN], ra.at[y], a_send.at[o], a_recv.at[YN - o], at_row(y_row(o)))

    for d in ZORDER[1:]:
        r = z_row(d)
        remote(block(r), block(r), z_send.at[d], z_recv.at[d], at_row(r)).wait_recv()
        to_y(0, d, 0, r)
        to_y(1, d, 0, r)
        to_sibling(0, d, 0, r)

    def last_leg(step, d):
        return d in ((0, 1) if step == 0 else (3, 2))

    def level(k):
        for d in ZORDER:
            for step in range(2):
                if k == YN // 2 and not last_leg(step, d):
                    continue
                r = source(step, d, k)
                remote(block(r), block(r), y_send.at[step, k, d], y_recv.at[step, k, d],
                       at_row(y_row(1))).wait_recv()
                if k < YN // 2 - 1 or (k == YN // 2 - 1 and last_leg(step, d)):
                    to_y(step, d, k, r)
                to_sibling(step, d, k, r)

    level(1)

    for o in range(1, YN):
        other = (y + o) % YN
        remote(ra.at[other], ra.at[other], a_send.at[o], a_recv.at[o], at_row(y_row(o))).wait_recv()
    part[...] = jnp.sum(ra[...], axis=0)
    rb[w] = part[...]
    for o in range(1, WN):
        send(part, rb.at[w], b_send.at[o], b_recv.at[WN - o], at_row(w_row(o)))

    level(2)

    for o in range(1, WN):
        other = (w + o) % WN
        remote(rb.at[other], rb.at[other], b_send.at[o], b_recv.at[o], at_row(w_row(o))).wait_recv()
    final[y] = jnp.sum(rb[...], axis=0)
    for o in range(1, YN):
        send(final.at[y], final.at[y], c_send.at[o], c_recv.at[YN - o], at_row(y_row(o)))

    level(3)
    level(4)

    for o in range(1, YN):
        other = (y + o) % YN
        remote(final.at[other], final.at[other], c_send.at[o], c_recv.at[o], at_row(y_row(o))).wait_recv()
    for q in range(YN):
        wg_out[(q // 2) * 8:(q // 2) * 8 + 8, (q % 2) * TILE:(q % 2 + 1) * TILE] = final[q]

    for k in range(YN // 2 + 1):
        for d in ZORDER:
            for step in range(1 if k == 0 else 2):
                if k == YN // 2 and not last_leg(step, d):
                    continue
                r = source(step, d, k) + 1 - 2 * core
                remote(block(r), block(r), s_send.at[step, k, d], s_recv.at[step, k, d],
                       at_row(sibling)).wait_recv()

    for load in loads[4:]:
        load.wait()
    in_use = count[0]
    first = row * BLOCKS
    group = 11
    total = jnp.zeros((BLOCKS * FEAT, TILE), jnp.float32)
    for g in range(0, SLOTS, group):
        pieces = []
        for t in range(g, g + group):
            here = x[coords[0, t]]
            j = jnp.where(t < in_use, coords[1, t] - first, -1)
            zero = jnp.zeros_like(here)
            pieces.append(jnp.concatenate(
                [jnp.where(j == b, here, zero) for b in range(BLOCKS)], axis=0))
        total += jnp.dot(
            jnp.concatenate(pieces, axis=1),
            tiles[g:g + group].reshape(group * TILE, TILE),
            preferred_element_type=jnp.float32,
        )
    for b in range(BLOCKS):
        fg_out[:, b * TILE:(b + 1) * TILE] = total[b * FEAT:(b + 1) * FEAT].astype(jnp.bfloat16)

    for copy in sends:
        copy.wait_send()


def shards(grad_out, pre_act, aggregated, weight, tiles, tile_coords, tile_count):
    bf16, f32 = jnp.bfloat16, jnp.float32
    vmem, dma = pltpu.VMEM, pltpu.SemaphoreType.DMA
    return pl.pallas_call(
        kernel,
        out_shape=(
            jax.ShapeDtypeStruct((FEAT, NODES), bf16),
            jax.ShapeDtypeStruct((FEAT, COLS * FEAT), f32),
        ),
        in_specs=[pl.BlockSpec(memory_space=pl.ANY)] * 7,
        out_specs=(pl.BlockSpec(memory_space=vmem), pl.BlockSpec(memory_space=vmem)),
        scratch_shapes=[
            vmem((FEAT, NODES), bf16),
            vmem((FEAT, NODES), bf16),
            vmem((FEAT, NODES), bf16),
            vmem((FEAT, COLS * FEAT), bf16),
            vmem((SLOTS, TILE, TILE), bf16),
            pltpu.SMEM((2, SLOTS), jnp.int32),
            pltpu.SMEM((1,), jnp.int32),
            vmem((COLS, FEAT, NODES), bf16),
            vmem((COLS, FEAT, TILE), bf16),
            vmem((TILE, COLS * FEAT), f32),
            vmem((ROWS * BLOCKS, FEAT, TILE), bf16),
            vmem((YN, 8, TILE), f32),
            vmem((YN, 8, TILE), f32),
            vmem((8, TILE), f32),
            vmem((WN, 8, TILE), f32),
            vmem((YN, 8, TILE), f32),
            dma((7,)),
            dma((COLS,)), dma((COLS,)), dma((COLS,)), dma((COLS,)),
            dma((ZN,)), dma((ZN,)),
            dma((2, 5, ZN)), dma((2, 5, ZN)),
            dma((2, 5, ZN)), dma((2, 5, ZN)),
            dma((YN,)), dma((YN,)), dma((WN,)), dma((WN,)), dma((YN,)), dma((YN,)),
        ],
        compiler_params=pltpu.CompilerParams(
            collective_id=0, has_side_effects=True, vmem_limit_bytes=32 * 1024 * 1024,
        ),
        cost_estimate=pl.CostEstimate(flops=300_000_000, bytes_accessed=6_000_000, transcendentals=0),
    )(grad_out, pre_act, aggregated, weight.T, tiles, tile_coords.T, tile_count)


def solution(mesh):
    in_specs = (
        P("col", "row"),
        P("col", "row"),
        P("col", "row"),
        P(None, "col"),
        P("row", None, None),
        P("row", None),
        P("row"),
    )
    out_specs = (P("col", "row"), P("col", None))
    return jax.shard_map(shards, mesh=mesh, in_specs=in_specs, out_specs=out_specs, check_vma=False)
```

```python
import jax
import jax.numpy as jnp
from jax import lax
from jax.experimental import pallas as pl
from jax.experimental.pallas import tpu as pltpu
from jax.sharding import PartitionSpec as P

YN, ZN, CORES, COLS = 8, 4, 2, 8
WN = ZN * CORES
ROWS = YN * WN
TILE = 128
BLOCKS = 4
FEAT = 32
NODES = BLOCKS * TILE
PARTS = 2
PART = BLOCKS // PARTS
PNODES = PART * TILE
SLOTS = 99
MESH = pl.DeviceIdType.MESH
SHEET = ((1, 2), (1, 1), (1, 3), (1, 0), (0, 2), (0, 1), (0, 3))


def kernel(
    go_hbm, pa_hbm, agg_hbm, wt_hbm, tiles_hbm, coords_hbm, count_hbm,
    fg_out, wg_out,
    go, pa, agg, wt, tiles, coords, count,
    masked, wpart, wrow, x, wl, ra, part, rb, final,
    in_sem, sent, w_recv, m_recv, z_recv, y_recv, s_recv, g_recv,
):
    row = lax.axis_index("row")
    col = lax.axis_index("col")
    y = row // WN
    w = row % WN
    z = w // CORES
    core = w % CORES
    sibling = row + 1 - 2 * core

    def col_of(dz, dx):
        return ((col // 4 + dz) % 2) * 4 + (col + dx) % 4

    def at_col(c):
        return {"row": row, "col": c}

    def at_row(r):
        return {"row": r, "col": col}

    def y_row(o):
        return ((y + o) % YN) * WN + w

    def w_row(o):
        return y * WN + (w + o) % WN

    def z_row(o):
        return y * WN + ((z + o) % ZN) * CORES + core

    loads = [
        pltpu.make_async_copy(src, dst, in_sem.at[n])
        for n, (src, dst) in enumerate((
            (go_hbm, go), (pa_hbm, pa), (wt_hbm, wt), (agg_hbm, agg),
            (coords_hbm, coords), (count_hbm, count), (tiles_hbm, tiles),
        ))
    ]
    for load in loads:
        load.start()

    barrier = pltpu.get_barrier_semaphore()
    for dz, dx in SHEET:
        pl.semaphore_signal(barrier, inc=1, device_id=at_col(col_of(dz, dx)), device_id_type=MESH)
    for o in range(1, YN):
        pl.semaphore_signal(barrier, inc=1, device_id=at_row(y_row(o)), device_id_type=MESH)
    for o in range(1, WN):
        pl.semaphore_signal(barrier, inc=1, device_id=at_row(w_row(o)), device_id_type=MESH)

    loads[0].wait()
    loads[1].wait()
    for h in range(PARTS):
        own_nodes = slice(h * PNODES, (h + 1) * PNODES)
        g = go[:, own_nodes]
        masked[h * COLS + col] = jnp.where(pa[:, own_nodes] > 0, g, jnp.zeros_like(g))
    loads[2].wait()
    wpart[col] = wt[:, pl.ds(pl.multiple_of((col // 4) * TILE, TILE), TILE)]

    pl.semaphore_wait(barrier, COLS - 1 + YN - 1 + WN - 1)

    def remote(src, dst, send, recv, to):
        return pltpu.make_async_remote_copy(
            src_ref=src, dst_ref=dst, send_sem=send, recv_sem=recv,
            device_id=to, device_id_type=MESH,
        )

    def send(src, dst, send_sem, recv_sem, to):
        remote(src, dst, send_sem, recv_sem, to).start()

    def arrived(ref, sem):
        pltpu.make_async_copy(ref, ref, sem).wait()

    y_sends = []

    others = COLS - 1
    for dz, dx in SHEET:
        peer = col_of(dz, dx)
        send(
            wt.at[:, pl.ds(pl.multiple_of((peer // 4) * TILE, TILE), TILE)],
            wpart.at[col], sent.at[0], w_recv.at[0], at_col(peer),
        )
    for h in range(PARTS):
        for dz, dx in SHEET:
            send(masked.at[h * COLS + col], masked.at[h * COLS + col], sent.at[1], m_recv.at[h],
                 at_col(col_of(dz, dx)))
    arrived(wpart.at[pl.ds(0, others)], w_recv.at[0])
    wrow[...] = wpart[...].reshape(COLS * FEAT, TILE).astype(jnp.float32).T
    own_w = wrow[pl.ds(pl.multiple_of((col % 4) * FEAT, FEAT), FEAT), :].astype(jnp.bfloat16)
    def part_of(r, h):
        return x.at[pl.ds(r * BLOCKS + h * PART, PART)]

    def to_y(step, d, h, k, far, r):
        send(part_of(r, h), part_of(r, h), sent.at[3], y_recv.at[far - 1, d, h],
             at_row(y_row((1 - 2 * step) * (far - k))))
        y_sends.append(far)

    def to_sibling(step, d, h, k, r):
        send(part_of(r, h), part_of(r, h), sent.at[4], s_recv.at[0], at_row(sibling))

    def source(step, d, k):
        return ((y - (1 - 2 * step) * k) % YN) * WN + ((z + d) % ZN) * CORES + core

    def masked_part(h):
        return masked[h * COLS:(h + 1) * COLS].reshape(COLS * FEAT, PNODES)

    for h in range(PARTS):
        arrived(masked.at[pl.ds(0, others)], m_recv.at[h])
        node_grad = jnp.dot(
            own_w, masked_part(h), preferred_element_type=jnp.float32
        ).astype(jnp.bfloat16)
        for b in range(PART):
            x[row * BLOCKS + h * PART + b] = node_grad[:, b * TILE:(b + 1) * TILE]
        to_y(0, 0, h, 0, 1, row)
        to_y(1, 0, h, 0, 1, row)
        for d in (1, 3, 2):
            send(part_of(row, h), part_of(row, h), sent.at[2], z_recv.at[ZN - d, h],
                 at_row(z_row(d)))
        to_sibling(0, 0, h, 0, row)

    loads[3].wait()
    wgrad = sum(
        lax.dot_general(
            agg[:, h * PNODES:(h + 1) * PNODES], masked_part(h),
            (((1,), (1,)), ((), ())), preferred_element_type=jnp.float32,
        )
        for h in range(PARTS)
    )
    for q in range(YN):
        piece = wgrad[(q // 2) * 8:(q // 2) * 8 + 8, (q % 2) * TILE:(q % 2 + 1) * TILE]
        wl[q] = piece
    ra[y] = wl[y]
    for o in range(1, YN):
        send(wl.at[(y + o) % YN], ra.at[y], sent.at[5], g_recv.at[0], at_row(y_row(o)))

    def from_z(d):
        r = z_row(d)
        for h in range(PARTS):
            arrived(part_of(r, h), z_recv.at[d, h])
            for far in (1, 2) if d == 2 else (1,):
                to_y(0, d, h, 0, far, r)
                to_y(1, d, h, 0, far, r)
            to_sibling(0, d, h, 0, r)

    def passed_on(step, d, k):
        if d == 2:
            return ((), (), (3,) if step == 0 else (3, 4), (), ())[k]
        return (k + 1,) if k < 3 or (k == 3 and last_leg(step, d)) else ()

    def last_leg(step, d):
        return step == (0 if d in (0, 1) else 1)

    def from_y(k, *ds):
        for d in ds:
            for h in range(PARTS):
                steps = [step for step in range(2) if k < YN // 2 or last_leg(step, d)]
                arrived(x.at[pl.ds(0, PART * len(steps))], y_recv.at[k - 1, d, h])
                for step in steps:
                    r = source(step, d, k)
                    for far in passed_on(step, d, k):
                        to_y(step, d, h, k, far, r)
                    to_sibling(step, d, h, k, r)

    from_y(1, 0)
    from_z(1)
    from_z(3)
    from_y(2, 0)

    arrived(ra.at[pl.ds(0, YN - 1)], g_recv.at[0])
    part[...] = jnp.sum(ra[...], axis=0)
    rb[w] = part[...]
    for o in range(1, WN):
        send(part, rb.at[w], sent.at[6], g_recv.at[1], at_row(w_row(o)))

    from_z(2)
    from_y(1, 1, 3)
    from_y(3, 0)
    from_y(1, 2)
    from_y(2, 1, 3)

    arrived(rb.at[pl.ds(0, WN - 1)], g_recv.at[1])
    final[y] = jnp.sum(rb[...], axis=0)
    for o in range(1, YN):
        send(final.at[y], final.at[y], sent.at[7], g_recv.at[2], at_row(y_row(o)))

    from_y(2, 2)
    from_y(4, 0)
    from_y(3, 1, 3, 2)
    from_y(4, 1, 3, 2)

    arrived(final.at[pl.ds(0, YN - 1)], g_recv.at[2])
    for q in range(YN):
        wg_out[(q // 2) * 8:(q // 2) * 8 + 8, (q % 2) * TILE:(q % 2 + 1) * TILE] = final[q]

    arrived(x.at[pl.ds(0, BLOCKS * ROWS // CORES)], s_recv.at[0])

    for load in loads[4:]:
        load.wait()
    in_use = count[0]
    first = row * BLOCKS
    group = 11
    total = jnp.zeros((BLOCKS * FEAT, TILE), jnp.float32)
    for g in range(0, SLOTS, group):
        pieces = []
        for t in range(g, g + group):
            here = x[coords[0, t]]
            j = jnp.where(t < in_use, coords[1, t] - first, -1)
            zero = jnp.zeros_like(here)
            pieces.append(jnp.concatenate(
                [jnp.where(j == b, here, zero) for b in range(BLOCKS)], axis=0))
        total += jnp.dot(
            jnp.concatenate(pieces, axis=1),
            tiles[g:g + group].reshape(group * TILE, TILE),
            preferred_element_type=jnp.float32,
        )
    for b in range(BLOCKS):
        fg_out[:, b * TILE:(b + 1) * TILE] = total[b * FEAT:(b + 1) * FEAT].astype(jnp.bfloat16)

    for n, ref in enumerate((
        wpart.at[pl.ds(0, others)], masked.at[pl.ds(0, PARTS * others)],
        x.at[pl.ds(0, (ZN - 1) * BLOCKS)], x.at[pl.ds(0, len(y_sends) * PART)],
        x.at[pl.ds(0, BLOCKS * ROWS // CORES)],
        wl.at[pl.ds(0, YN - 1)], rb.at[pl.ds(0, WN - 1)], final.at[pl.ds(0, YN - 1)],
    )):
        arrived(ref, sent.at[n])


def shards(grad_out, pre_act, aggregated, weight, tiles, tile_coords, tile_count):
    bf16, f32 = jnp.bfloat16, jnp.float32
    vmem, dma = pltpu.VMEM, pltpu.SemaphoreType.DMA
    return pl.pallas_call(
        kernel,
        out_shape=(
            jax.ShapeDtypeStruct((FEAT, NODES), bf16),
            jax.ShapeDtypeStruct((FEAT, COLS * FEAT), f32),
        ),
        in_specs=[pl.BlockSpec(memory_space=pl.ANY)] * 7,
        out_specs=(pl.BlockSpec(memory_space=vmem), pl.BlockSpec(memory_space=vmem)),
        scratch_shapes=[
            vmem((FEAT, NODES), bf16),
            vmem((FEAT, NODES), bf16),
            vmem((FEAT, NODES), bf16),
            vmem((FEAT, COLS * FEAT), bf16),
            vmem((SLOTS, TILE, TILE), bf16),
            pltpu.SMEM((2, SLOTS), jnp.int32),
            pltpu.SMEM((1,), jnp.int32),
            vmem((PARTS * COLS, FEAT, PNODES), bf16),
            vmem((COLS, FEAT, TILE), bf16),
            vmem((TILE, COLS * FEAT), f32),
            vmem((ROWS * BLOCKS, FEAT, TILE), bf16),
            vmem((YN, 8, TILE), f32),
            vmem((YN, 8, TILE), f32),
            vmem((8, TILE), f32),
            vmem((WN, 8, TILE), f32),
            vmem((YN, 8, TILE), f32),
            dma((7,)),
            dma((8,)), dma((1,)), dma((PARTS,)), dma((ZN, PARTS)), dma((YN // 2, ZN, PARTS)), dma((1,)), dma((3,)),
        ],
        compiler_params=pltpu.CompilerParams(
            collective_id=0, has_side_effects=True, vmem_limit_bytes=60 * 1024 * 1024,
        ),
        cost_estimate=pl.CostEstimate(flops=300_000_000, bytes_accessed=6_000_000, transcendentals=0),
    )(grad_out, pre_act, aggregated, weight.T, tiles, tile_coords.T, tile_count)


def solution(mesh):
    in_specs = (
        P("col", "row"),
        P("col", "row"),
        P("col", "row"),
        P(None, "col"),
        P("row", None, None),
        P("row", None),
        P("row"),
    )
    out_specs = (P("col", "row"), P("col", None))
    return jax.shard_map(shards, mesh=mesh, in_specs=in_specs, out_specs=out_specs, check_vma=False)
```

```python
import jax
import jax.numpy as jnp
from jax import lax
from jax.experimental import pallas as pl
from jax.experimental.pallas import tpu as pltpu
from jax.sharding import PartitionSpec as P

YN, ZN, CORES, COLS = 8, 4, 2, 8
WN = ZN * CORES
ROWS = YN * WN
TILE = 128
BLOCKS = 4
FEAT = 32
NODES = BLOCKS * TILE
PARTS = 2
PART = BLOCKS // PARTS
PNODES = PART * TILE
SLOTS = 99
MESH = pl.DeviceIdType.MESH
SHEET = ((1, 2), (1, 1), (1, 3), (1, 0), (0, 2), (0, 1), (0, 3))


def kernel(
    go_hbm, pa_hbm, agg_hbm, wt_hbm, tiles_hbm, coords_hbm, count_hbm,
    fg_out, wg_out,
    go, pa, agg, wt, tiles, coords, count,
    masked, wpart, wrow, x, wl, ra, part, rb, final,
    in_sem, sent, w_recv, m_recv, z_recv, y_recv, s_recv, g_recv,
):
    row = lax.axis_index("row")
    col = lax.axis_index("col")
    y = row // WN
    w = row % WN
    z = w // CORES
    core = w % CORES
    sibling = row + 1 - 2 * core

    def col_of(dz, dx):
        return ((col // 4 + dz) % 2) * 4 + (col + dx) % 4

    def at_col(c):
        return {"row": row, "col": c}

    def at_row(r):
        return {"row": r, "col": col}

    def y_row(o):
        return ((y + o) % YN) * WN + w

    def w_row(o):
        return y * WN + (w + o) % WN

    def z_row(o):
        return y * WN + ((z + o) % ZN) * CORES + core

    loads = [
        pltpu.make_async_copy(src, dst, in_sem.at[n])
        for n, (src, dst) in enumerate((
            (go_hbm, go), (pa_hbm, pa), (wt_hbm, wt), (agg_hbm, agg),
            (coords_hbm, coords), (count_hbm, count), (tiles_hbm, tiles),
        ))
    ]
    for load in loads:
        load.start()

    barrier = pltpu.get_barrier_semaphore()
    for dz, dx in SHEET:
        pl.semaphore_signal(barrier, inc=1, device_id=at_col(col_of(dz, dx)), device_id_type=MESH)
    for o in range(1, YN):
        pl.semaphore_signal(barrier, inc=1, device_id=at_row(y_row(o)), device_id_type=MESH)
    for o in range(1, WN):
        pl.semaphore_signal(barrier, inc=1, device_id=at_row(w_row(o)), device_id_type=MESH)

    loads[0].wait()
    loads[1].wait()
    for h in range(PARTS):
        own_nodes = slice(h * PNODES, (h + 1) * PNODES)
        g = go[:, own_nodes]
        masked[h * COLS + col] = jnp.where(pa[:, own_nodes] > 0, g, jnp.zeros_like(g))
    loads[2].wait()
    wpart[col] = wt[:, pl.ds(pl.multiple_of((col // 4) * TILE, TILE), TILE)]

    pl.semaphore_wait(barrier, COLS - 1 + YN - 1 + WN - 1)

    def remote(src, dst, send, recv, to):
        return pltpu.make_async_remote_copy(
            src_ref=src, dst_ref=dst, send_sem=send, recv_sem=recv,
            device_id=to, device_id_type=MESH,
        )

    def send(src, dst, send_sem, recv_sem, to):
        remote(src, dst, send_sem, recv_sem, to).start()

    def arrived(ref, sem):
        pltpu.make_async_copy(ref, ref, sem).wait()

    y_sends, z_sends = [], []

    others = COLS - 1
    for dz, dx in SHEET:
        peer = col_of(dz, dx)
        send(
            wt.at[:, pl.ds(pl.multiple_of((peer // 4) * TILE, TILE), TILE)],
            wpart.at[col], sent.at[0], w_recv.at[0], at_col(peer),
        )
    for h in range(PARTS):
        for dz, dx in SHEET:
            send(masked.at[h * COLS + col], masked.at[h * COLS + col], sent.at[1], m_recv.at[h],
                 at_col(col_of(dz, dx)))
    arrived(wpart.at[pl.ds(0, others)], w_recv.at[0])
    wrow[...] = wpart[...].reshape(COLS * FEAT, TILE).astype(jnp.float32).T
    own_w = wrow[pl.ds(pl.multiple_of((col % 4) * FEAT, FEAT), FEAT), :].astype(jnp.bfloat16)
    def part_of(r, h):
        return x.at[pl.ds(r * BLOCKS + h * PART, PART)]

    def to_y(step, d, h, k, far, r):
        send(part_of(r, h), part_of(r, h), sent.at[3], y_recv.at[far - 1, d, h],
             at_row(y_row((1 - 2 * step) * (far - k))))
        y_sends.append(far)

    def to_z(d, h, r, sem):
        send(part_of(r, h), part_of(r, h), sent.at[2], sem, at_row(z_row(d)))
        z_sends.append(d)

    def to_sibling(step, d, h, k, r):
        send(part_of(r, h), part_of(r, h), sent.at[4], s_recv.at[0], at_row(sibling))

    def source(step, d, k):
        return ((y - (1 - 2 * step) * k) % YN) * WN + ((z + d) % ZN) * CORES + core

    def masked_part(h):
        return masked[h * COLS:(h + 1) * COLS].reshape(COLS * FEAT, PNODES)

    for h in range(PARTS):
        arrived(masked.at[pl.ds(0, others)], m_recv.at[h])
        node_grad = jnp.dot(
            own_w, masked_part(h), preferred_element_type=jnp.float32
        ).astype(jnp.bfloat16)
        for b in range(PART):
            x[row * BLOCKS + h * PART + b] = node_grad[:, b * TILE:(b + 1) * TILE]
        for far in (1, 2):
            for step in range(2):
                to_y(step, 0, h, 0, far, row)
        for d in (1, 3, 2):
            to_z(d, h, row, z_recv.at[ZN - d, h])
        to_sibling(0, 0, h, 0, row)

    loads[3].wait()
    wgrad = sum(
        lax.dot_general(
            agg[:, h * PNODES:(h + 1) * PNODES], masked_part(h),
            (((1,), (1,)), ((), ())), preferred_element_type=jnp.float32,
        )
        for h in range(PARTS)
    )
    for q in range(YN):
        piece = wgrad[(q // 2) * 8:(q // 2) * 8 + 8, (q % 2) * TILE:(q % 2 + 1) * TILE]
        wl[q] = piece
    ra[y] = wl[y]
    for o in range(1, YN):
        send(wl.at[(y + o) % YN], ra.at[y], sent.at[5], g_recv.at[0], at_row(y_row(o)))

    def from_z(d):
        r = z_row(d)
        for h in range(PARTS):
            arrived(part_of(r, h), z_recv.at[d, h])
            for far in (1, 2) if d == 2 else (1,):
                to_y(0, d, h, 0, far, r)
                to_y(1, d, h, 0, far, r)
            to_sibling(0, d, h, 0, r)

    def passed_on(step, d, k):
        if d in (1, 3):
            return (2,) if k == 1 else ()
        return () if k != 2 else (3, 4) if last_leg(step, d) else (3,)

    def last_leg(step, d):
        return step == (0 if d in (0, 1) else 1)

    def from_y(k, *ds):
        for d in ds:
            for h in range(PARTS):
                steps = [step for step in range(2) if k < YN // 2 or last_leg(step, d)]
                arrived(x.at[pl.ds(0, PART * len(steps))], y_recv.at[k - 1, d, h])
                for step in steps:
                    r = source(step, d, k)
                    for far in passed_on(step, d, k):
                        to_y(step, d, h, k, far, r)
                    if d == 0 and k > 2:
                        for o in (1, 3):
                            to_z(o, h, r, y_recv.at[k - 1, ZN - o, h])
                    to_sibling(step, d, h, k, r)

    from_y(1, 0)
    from_y(2, 0)
    from_z(1)
    from_z(3)

    arrived(ra.at[pl.ds(0, YN - 1)], g_recv.at[0])
    part[...] = jnp.sum(ra[...], axis=0)
    rb[w] = part[...]
    for o in range(1, WN):
        send(part, rb.at[w], sent.at[6], g_recv.at[1], at_row(w_row(o)))

    from_y(3, 0)
    from_z(2)
    from_y(1, 1, 3)
    from_y(4, 0)
    from_y(1, 2)
    from_y(2, 2)

    arrived(rb.at[pl.ds(0, WN - 1)], g_recv.at[1])
    final[y] = jnp.sum(rb[...], axis=0)
    for o in range(1, YN):
        send(final.at[y], final.at[y], sent.at[7], g_recv.at[2], at_row(y_row(o)))

    from_y(2, 1, 3)
    from_y(3, 1, 3)
    from_y(4, 1, 3)
    from_y(3, 2)
    from_y(4, 2)

    arrived(final.at[pl.ds(0, YN - 1)], g_recv.at[2])
    for q in range(YN):
        wg_out[(q // 2) * 8:(q // 2) * 8 + 8, (q % 2) * TILE:(q % 2 + 1) * TILE] = final[q]

    arrived(x.at[pl.ds(0, BLOCKS * ROWS // CORES)], s_recv.at[0])

    for load in loads[4:]:
        load.wait()
    in_use = count[0]
    first = row * BLOCKS
    group = 11
    total = jnp.zeros((BLOCKS * FEAT, TILE), jnp.float32)
    for g in range(0, SLOTS, group):
        pieces = []
        for t in range(g, g + group):
            here = x[coords[0, t]]
            j = jnp.where(t < in_use, coords[1, t] - first, -1)
            zero = jnp.zeros_like(here)
            pieces.append(jnp.concatenate(
                [jnp.where(j == b, here, zero) for b in range(BLOCKS)], axis=0))
        total += jnp.dot(
            jnp.concatenate(pieces, axis=1),
            tiles[g:g + group].reshape(group * TILE, TILE),
            preferred_element_type=jnp.float32,
        )
    for b in range(BLOCKS):
        fg_out[:, b * TILE:(b + 1) * TILE] = total[b * FEAT:(b + 1) * FEAT].astype(jnp.bfloat16)

    for n, ref in enumerate((
        wpart.at[pl.ds(0, others)], masked.at[pl.ds(0, PARTS * others)],
        x.at[pl.ds(0, len(z_sends) * PART)], x.at[pl.ds(0, len(y_sends) * PART)],
        x.at[pl.ds(0, BLOCKS * ROWS // CORES)],
        wl.at[pl.ds(0, YN - 1)], rb.at[pl.ds(0, WN - 1)], final.at[pl.ds(0, YN - 1)],
    )):
        arrived(ref, sent.at[n])


def shards(grad_out, pre_act, aggregated, weight, tiles, tile_coords, tile_count):
    bf16, f32 = jnp.bfloat16, jnp.float32
    vmem, dma = pltpu.VMEM, pltpu.SemaphoreType.DMA
    return pl.pallas_call(
        kernel,
        out_shape=(
            jax.ShapeDtypeStruct((FEAT, NODES), bf16),
            jax.ShapeDtypeStruct((FEAT, COLS * FEAT), f32),
        ),
        in_specs=[pl.BlockSpec(memory_space=pl.ANY)] * 7,
        out_specs=(pl.BlockSpec(memory_space=vmem), pl.BlockSpec(memory_space=vmem)),
        scratch_shapes=[
            vmem((FEAT, NODES), bf16),
            vmem((FEAT, NODES), bf16),
            vmem((FEAT, NODES), bf16),
            vmem((FEAT, COLS * FEAT), bf16),
            vmem((SLOTS, TILE, TILE), bf16),
            pltpu.SMEM((2, SLOTS), jnp.int32),
            pltpu.SMEM((1,), jnp.int32),
            vmem((PARTS * COLS, FEAT, PNODES), bf16),
            vmem((COLS, FEAT, TILE), bf16),
            vmem((TILE, COLS * FEAT), f32),
            vmem((ROWS * BLOCKS, FEAT, TILE), bf16),
            vmem((YN, 8, TILE), f32),
            vmem((YN, 8, TILE), f32),
            vmem((8, TILE), f32),
            vmem((WN, 8, TILE), f32),
            vmem((YN, 8, TILE), f32),
            dma((7,)),
            dma((8,)), dma((1,)), dma((PARTS,)), dma((ZN, PARTS)), dma((YN // 2, ZN, PARTS)), dma((1,)), dma((3,)),
        ],
        compiler_params=pltpu.CompilerParams(
            collective_id=0, has_side_effects=True, vmem_limit_bytes=60 * 1024 * 1024,
        ),
        cost_estimate=pl.CostEstimate(flops=300_000_000, bytes_accessed=6_000_000, transcendentals=0),
    )(grad_out, pre_act, aggregated, weight.T, tiles, tile_coords.T, tile_count)


def solution(mesh):
    in_specs = (
        P("col", "row"),
        P("col", "row"),
        P("col", "row"),
        P(None, "col"),
        P("row", None, None),
        P("row", None),
        P("row"),
    )
    out_specs = (P("col", "row"), P("col", None))
    return jax.shard_map(shards, mesh=mesh, in_specs=in_specs, out_specs=out_specs, check_vma=False)
```

```python
import jax
import jax.numpy as jnp
from jax import lax
from jax.experimental import pallas as pl
from jax.experimental.pallas import tpu as pltpu
from jax.sharding import PartitionSpec as P

YN, ZN, CORES, COLS = 8, 4, 2, 8
WN = ZN * CORES
ROWS = YN * WN
TILE = 128
BLOCKS = 4
FEAT = 32
NODES = BLOCKS * TILE
PARTS = 2
PART = BLOCKS // PARTS
PNODES = PART * TILE
SLOTS = 99
MESH = pl.DeviceIdType.MESH
SHEET = ((1, 2), (1, 1), (1, 3), (1, 0), (0, 2), (0, 1), (0, 3))


def kernel(
    go_hbm, pa_hbm, agg_hbm, wt_hbm, tiles_hbm, coords_hbm, count_hbm,
    fg_out, wg_out,
    go, pa, agg, wt, tiles, coords, count,
    masked, wpart, wrow, x, wl, ra, part, rb, final,
    in_sem, sent, w_recv, m_recv, z_recv, y_recv, s_recv, g_recv,
):
    row = lax.axis_index("row")
    col = lax.axis_index("col")
    y = row // WN
    w = row % WN
    z = w // CORES
    core = w % CORES
    sibling = row + 1 - 2 * core

    def col_of(dz, dx):
        return ((col // 4 + dz) % 2) * 4 + (col + dx) % 4

    def at_col(c):
        return {"row": row, "col": c}

    def at_row(r):
        return {"row": r, "col": col}

    def y_row(o):
        return ((y + o) % YN) * WN + w

    def w_row(o):
        return y * WN + (w + o) % WN

    def z_row(o):
        return y * WN + ((z + o) % ZN) * CORES + core

    loads = [
        pltpu.make_async_copy(src, dst, in_sem.at[n])
        for n, (src, dst) in enumerate((
            (go_hbm, go), (pa_hbm, pa), (wt_hbm, wt), (agg_hbm, agg),
            (coords_hbm, coords), (count_hbm, count), (tiles_hbm, tiles),
        ))
    ]
    for load in loads:
        load.start()

    barrier = pltpu.get_barrier_semaphore()
    for dz, dx in SHEET:
        pl.semaphore_signal(barrier, inc=1, device_id=at_col(col_of(dz, dx)), device_id_type=MESH)
    for o in range(1, YN):
        pl.semaphore_signal(barrier, inc=1, device_id=at_row(y_row(o)), device_id_type=MESH)
    for o in range(1, WN):
        pl.semaphore_signal(barrier, inc=1, device_id=at_row(w_row(o)), device_id_type=MESH)

    loads[0].wait()
    loads[1].wait()
    for h in range(PARTS):
        own_nodes = slice(h * PNODES, (h + 1) * PNODES)
        g = go[:, own_nodes]
        masked[h * COLS + col] = jnp.where(pa[:, own_nodes] > 0, g, jnp.zeros_like(g))
    loads[2].wait()
    wpart[col] = wt[:, pl.ds(pl.multiple_of((col // 4) * TILE, TILE), TILE)]

    pl.semaphore_wait(barrier, COLS - 1 + YN - 1 + WN - 1)

    def remote(src, dst, send, recv, to):
        return pltpu.make_async_remote_copy(
            src_ref=src, dst_ref=dst, send_sem=send, recv_sem=recv,
            device_id=to, device_id_type=MESH,
        )

    def send(src, dst, send_sem, recv_sem, to):
        remote(src, dst, send_sem, recv_sem, to).start()

    def arrived(ref, sem):
        pltpu.make_async_copy(ref, ref, sem).wait()

    y_sends, z_sends = [], []

    others = COLS - 1
    for dz, dx in SHEET:
        peer = col_of(dz, dx)
        send(
            wt.at[:, pl.ds(pl.multiple_of((peer // 4) * TILE, TILE), TILE)],
            wpart.at[col], sent.at[0], w_recv.at[0], at_col(peer),
        )
    for h in range(PARTS):
        for dz, dx in SHEET:
            send(masked.at[h * COLS + col], masked.at[h * COLS + col], sent.at[1], m_recv.at[h],
                 at_col(col_of(dz, dx)))
    arrived(wpart.at[pl.ds(0, others)], w_recv.at[0])
    wrow[...] = wpart[...].reshape(COLS * FEAT, TILE).astype(jnp.float32).T
    own_w = wrow[pl.ds(pl.multiple_of((col % 4) * FEAT, FEAT), FEAT), :].astype(jnp.bfloat16)
    def part_of(r, h):
        return x.at[pl.ds(r * BLOCKS + h * PART, PART)]

    def to_y(step, d, h, k, far, r):
        send(part_of(r, h), part_of(r, h), sent.at[3], y_recv.at[far - 1, d, h],
             at_row(y_row((1 - 2 * step) * (far - k))))
        y_sends.append(far)

    def to_z(d, h, r, sem):
        send(part_of(r, h), part_of(r, h), sent.at[2], sem, at_row(z_row(d)))
        z_sends.append(d)

    def to_sibling(step, d, h, k, r):
        send(part_of(r, h), part_of(r, h), sent.at[4], s_recv.at[0], at_row(sibling))

    def source(step, d, k):
        return ((y - (1 - 2 * step) * k) % YN) * WN + ((z + d) % ZN) * CORES + core

    def masked_part(h):
        return masked[h * COLS:(h + 1) * COLS].reshape(COLS * FEAT, PNODES)

    for h in range(PARTS):
        arrived(masked.at[pl.ds(0, others)], m_recv.at[h])
        node_grad = jnp.dot(
            own_w, masked_part(h), preferred_element_type=jnp.float32
        ).astype(jnp.bfloat16)
        for b in range(PART):
            x[row * BLOCKS + h * PART + b] = node_grad[:, b * TILE:(b + 1) * TILE]
        for far in (1, 2):
            for step in range(2):
                to_y(step, 0, h, 0, far, row)
        for d in (1, 3, 2):
            to_z(d, h, row, z_recv.at[ZN - d, h])
        to_sibling(0, 0, h, 0, row)

    loads[3].wait()
    wgrad = sum(
        lax.dot_general(
            agg[:, h * PNODES:(h + 1) * PNODES], masked_part(h),
            (((1,), (1,)), ((), ())), preferred_element_type=jnp.float32,
        )
        for h in range(PARTS)
    )
    for q in range(YN):
        piece = wgrad[(q // 2) * 8:(q // 2) * 8 + 8, (q % 2) * TILE:(q % 2 + 1) * TILE]
        wl[q] = piece
    ra[y] = wl[y]
    for o in range(1, YN):
        send(wl.at[(y + o) % YN], ra.at[y], sent.at[5], g_recv.at[0], at_row(y_row(o)))

    def from_z(d):
        r = z_row(d)
        for h in range(PARTS):
            arrived(part_of(r, h), z_recv.at[d, h])
            for far in (1, 2) if d == 2 else (1,):
                to_y(0, d, h, 0, far, r)
                to_y(1, d, h, 0, far, r)
            to_sibling(0, d, h, 0, r)

    def passed_on(step, d, k):
        if d in (1, 3):
            return (2,) if k == 1 else ()
        return () if k != 2 else (3, 4) if last_leg(step, d) else (3,)

    def last_leg(step, d):
        return step == (0 if d in (0, 1) else 1)

    def from_y(k, *ds):
        for d in ds:
            for h in range(PARTS):
                steps = [step for step in range(2) if k < YN // 2 or last_leg(step, d)]
                arrived(x.at[pl.ds(0, PART * len(steps))], y_recv.at[k - 1, d, h])
                for step in steps:
                    r = source(step, d, k)
                    for far in passed_on(step, d, k):
                        to_y(step, d, h, k, far, r)
                    if d == 0 and k > 2:
                        for o in (1, 3):
                            to_z(o, h, r, y_recv.at[k - 1, ZN - o, h])
                    to_sibling(step, d, h, k, r)

    from_y(1, 0)
    from_y(2, 0)
    from_z(1)
    from_z(3)

    arrived(ra.at[pl.ds(0, YN - 1)], g_recv.at[0])
    part[...] = jnp.sum(ra[...], axis=0)
    rb[w] = part[...]
    for o in range(1, WN):
        send(part, rb.at[w], sent.at[6], g_recv.at[1], at_row(w_row(o)))

    from_y(3, 0)
    from_z(2)
    from_y(1, 1, 3)
    from_y(4, 0)
    from_y(1, 2)
    from_y(2, 2)

    arrived(rb.at[pl.ds(0, WN - 1)], g_recv.at[1])
    final[y] = jnp.sum(rb[...], axis=0)
    for o in range(1, YN):
        send(final.at[y], final.at[y], sent.at[7], g_recv.at[2], at_row(y_row(o)))

    from_y(2, 1, 3)
    from_y(3, 1, 3)
    from_y(4, 1, 3)
    from_y(3, 2)
    from_y(4, 2)

    arrived(final.at[pl.ds(0, YN - 1)], g_recv.at[2])
    for q in range(YN):
        wg_out[(q // 2) * 8:(q // 2) * 8 + 8, (q % 2) * TILE:(q % 2 + 1) * TILE] = final[q]

    arrived(x.at[pl.ds(0, BLOCKS * ROWS // CORES)], s_recv.at[0])

    for load in loads[4:]:
        load.wait()
    in_use = count[0]
    first = row * BLOCKS
    group = 11
    total = jnp.zeros((BLOCKS * FEAT, TILE), jnp.float32)
    for g in range(0, SLOTS, group):
        pieces = []
        for t in range(g, g + group):
            here = x[coords[0, t]]
            j = jnp.where(t < in_use, coords[1, t] - first, -1)
            zero = jnp.zeros_like(here)
            pieces.append(jnp.concatenate(
                [jnp.where(j == b, here, zero) for b in range(BLOCKS)], axis=0))
        total += jnp.dot(
            jnp.concatenate(pieces, axis=1),
            tiles[g:g + group].reshape(group * TILE, TILE),
            preferred_element_type=jnp.float32,
        )
    for b in range(BLOCKS):
        fg_out[:, b * TILE:(b + 1) * TILE] = total[b * FEAT:(b + 1) * FEAT].astype(jnp.bfloat16)

    for n, ref in enumerate((
        wpart.at[pl.ds(0, others)], masked.at[pl.ds(0, PARTS * others)],
        x.at[pl.ds(0, len(z_sends) * PART)], x.at[pl.ds(0, len(y_sends) * PART)],
        x.at[pl.ds(0, BLOCKS * ROWS // CORES)],
        wl.at[pl.ds(0, YN - 1)], rb.at[pl.ds(0, WN - 1)], final.at[pl.ds(0, YN - 1)],
    )):
        arrived(ref, sent.at[n])


def shards(grad_out, pre_act, aggregated, weight, tiles, tile_coords, tile_count):
    bf16, f32 = jnp.bfloat16, jnp.float32
    vmem, dma = pltpu.VMEM, pltpu.SemaphoreType.DMA
    return pl.pallas_call(
        kernel,
        out_shape=(
            vmem((FEAT, NODES), bf16),
            vmem((FEAT, COLS * FEAT), f32),
        ),
        in_specs=[pl.BlockSpec(memory_space=pl.ANY)] * 7,
        out_specs=(pl.BlockSpec(memory_space=vmem), pl.BlockSpec(memory_space=vmem)),
        scratch_shapes=[
            vmem((FEAT, NODES), bf16),
            vmem((FEAT, NODES), bf16),
            vmem((FEAT, NODES), bf16),
            vmem((FEAT, COLS * FEAT), bf16),
            vmem((SLOTS, TILE, TILE), bf16),
            pltpu.SMEM((2, SLOTS), jnp.int32),
            pltpu.SMEM((1,), jnp.int32),
            vmem((PARTS * COLS, FEAT, PNODES), bf16),
            vmem((COLS, FEAT, TILE), bf16),
            vmem((TILE, COLS * FEAT), f32),
            vmem((ROWS * BLOCKS, FEAT, TILE), bf16),
            vmem((YN, 8, TILE), f32),
            vmem((YN, 8, TILE), f32),
            vmem((8, TILE), f32),
            vmem((WN, 8, TILE), f32),
            vmem((YN, 8, TILE), f32),
            dma((7,)),
            dma((8,)), dma((1,)), dma((PARTS,)), dma((ZN, PARTS)), dma((YN // 2, ZN, PARTS)), dma((1,)), dma((3,)),
        ],
        compiler_params=pltpu.CompilerParams(
            collective_id=0, has_side_effects=True, vmem_limit_bytes=55168 * 1024,
        ),
        cost_estimate=pl.CostEstimate(flops=300_000_000, bytes_accessed=6_000_000, transcendentals=0),
    )(grad_out, pre_act, aggregated, weight.T, tiles, tile_coords.T, tile_count)


def solution(mesh):
    in_specs = (
        P("col", "row"),
        P("col", "row"),
        P("col", "row"),
        P(None, "col"),
        P("row", None, None),
        P("row", None),
        P("row"),
    )
    out_specs = (P("col", "row"), P("col", None))
    return jax.shard_map(shards, mesh=mesh, in_specs=in_specs, out_specs=out_specs, check_vma=False)
```

```python
import jax
import jax.numpy as jnp
from jax import lax
from jax.experimental import pallas as pl
from jax.experimental.pallas import tpu as pltpu
from jax.sharding import PartitionSpec as P

YN, ZN, CORES, COLS = 8, 4, 2, 8
WN = ZN * CORES
ROWS = YN * WN
TILE = 128
BLOCKS = 4
FEAT = 32
NODES = BLOCKS * TILE
PARTS = 1
PART = BLOCKS // PARTS
PNODES = PART * TILE
SLOTS = 99
MESH = pl.DeviceIdType.MESH
SHEET = ((1, 2), (1, 1), (1, 3), (1, 0), (0, 2), (0, 1), (0, 3))


def kernel(
    go_hbm, pa_hbm, agg_hbm, wt_hbm, tiles_hbm, coords_hbm, count_hbm,
    fg_out, wg_out,
    go, pa, agg, wt, tiles, coords, count,
    masked, wpart, wrow, x, wl, ra, part, rb, final,
    in_sem, sent, w_recv, m_recv, z_recv, y_recv, s_recv, g_recv,
):
    row = lax.axis_index("row")
    col = lax.axis_index("col")
    y = row // WN
    w = row % WN
    z = w // CORES
    core = w % CORES
    sibling = row + 1 - 2 * core

    def col_of(dz, dx):
        return ((col // 4 + dz) % 2) * 4 + (col + dx) % 4

    def at_col(c):
        return {"row": row, "col": c}

    def at_row(r):
        return {"row": r, "col": col}

    def y_row(o):
        return ((y + o) % YN) * WN + w

    def w_row(o):
        return y * WN + (w + o) % WN

    def z_row(o):
        return y * WN + ((z + o) % ZN) * CORES + core

    loads = [
        pltpu.make_async_copy(src, dst, in_sem.at[n])
        for n, (src, dst) in enumerate((
            (go_hbm, go), (pa_hbm, pa), (wt_hbm, wt), (agg_hbm, agg),
            (coords_hbm, coords), (count_hbm, count), (tiles_hbm, tiles),
        ))
    ]
    for load in loads:
        load.start()

    barrier = pltpu.get_barrier_semaphore()
    for dz, dx in SHEET:
        pl.semaphore_signal(barrier, inc=1, device_id=at_col(col_of(dz, dx)), device_id_type=MESH)
    for o in range(1, YN):
        pl.semaphore_signal(barrier, inc=1, device_id=at_row(y_row(o)), device_id_type=MESH)
    for o in range(1, WN):
        pl.semaphore_signal(barrier, inc=1, device_id=at_row(w_row(o)), device_id_type=MESH)

    loads[0].wait()
    loads[1].wait()
    for h in range(PARTS):
        own_nodes = slice(h * PNODES, (h + 1) * PNODES)
        g = go[:, own_nodes]
        masked[h * COLS + col] = jnp.where(pa[:, own_nodes] > 0, g, jnp.zeros_like(g))
    loads[2].wait()
    wpart[col] = wt[:, pl.ds(pl.multiple_of((col // 4) * TILE, TILE), TILE)]

    pl.semaphore_wait(barrier, COLS - 1 + YN - 1 + WN - 1)

    def remote(src, dst, send, recv, to):
        return pltpu.make_async_remote_copy(
            src_ref=src, dst_ref=dst, send_sem=send, recv_sem=recv,
            device_id=to, device_id_type=MESH,
        )

    def send(src, dst, send_sem, recv_sem, to):
        remote(src, dst, send_sem, recv_sem, to).start()

    def arrived(ref, sem):
        pltpu.make_async_copy(ref, ref, sem).wait()

    y_sends, z_sends = [], []

    others = COLS - 1
    for dz, dx in SHEET:
        peer = col_of(dz, dx)
        send(
            wt.at[:, pl.ds(pl.multiple_of((peer // 4) * TILE, TILE), TILE)],
            wpart.at[col], sent.at[0], w_recv.at[0], at_col(peer),
        )
    for h in range(PARTS):
        for dz, dx in SHEET:
            send(masked.at[h * COLS + col], masked.at[h * COLS + col], sent.at[1], m_recv.at[h],
                 at_col(col_of(dz, dx)))
    arrived(wpart.at[pl.ds(0, others)], w_recv.at[0])
    wrow[...] = wpart[...].reshape(COLS * FEAT, TILE).astype(jnp.float32).T
    own_w = wrow[pl.ds(pl.multiple_of((col % 4) * FEAT, FEAT), FEAT), :].astype(jnp.bfloat16)
    def part_of(r, h):
        return x.at[pl.ds(r * BLOCKS + h * PART, PART)]

    def to_y(step, d, h, k, far, r):
        send(part_of(r, h), part_of(r, h), sent.at[3], y_recv.at[far - 1, d, h],
             at_row(y_row((1 - 2 * step) * (far - k))))
        y_sends.append(far)

    def to_z(d, h, r, sem):
        send(part_of(r, h), part_of(r, h), sent.at[2], sem, at_row(z_row(d)))
        z_sends.append(d)

    def to_sibling(step, d, h, k, r):
        send(part_of(r, h), part_of(r, h), sent.at[4], s_recv.at[0], at_row(sibling))

    def source(step, d, k):
        return ((y - (1 - 2 * step) * k) % YN) * WN + ((z + d) % ZN) * CORES + core

    def masked_part(h):
        return masked[h * COLS:(h + 1) * COLS].reshape(COLS * FEAT, PNODES)

    for h in range(PARTS):
        arrived(masked.at[pl.ds(0, others)], m_recv.at[h])
        node_grad = jnp.dot(
            own_w, masked_part(h), preferred_element_type=jnp.float32
        ).astype(jnp.bfloat16)
        for b in range(PART):
            x[row * BLOCKS + h * PART + b] = node_grad[:, b * TILE:(b + 1) * TILE]
        for far in (1, 2):
            for step in range(2):
                to_y(step, 0, h, 0, far, row)
        for d in (1, 3, 2):
            to_z(d, h, row, z_recv.at[ZN - d, h])
        to_sibling(0, 0, h, 0, row)

    loads[3].wait()
    wgrad = sum(
        lax.dot_general(
            agg[:, h * PNODES:(h + 1) * PNODES], masked_part(h),
            (((1,), (1,)), ((), ())), preferred_element_type=jnp.float32,
        )
        for h in range(PARTS)
    )
    for q in range(YN):
        piece = wgrad[(q // 2) * 8:(q // 2) * 8 + 8, (q % 2) * TILE:(q % 2 + 1) * TILE]
        wl[q] = piece
    ra[y] = wl[y]
    for o in range(1, YN):
        send(wl.at[(y + o) % YN], ra.at[y], sent.at[5], g_recv.at[0], at_row(y_row(o)))

    def from_z(d):
        r = z_row(d)
        for h in range(PARTS):
            arrived(part_of(r, h), z_recv.at[d, h])
            for far in (1, 2) if d == 2 else (1,):
                to_y(0, d, h, 0, far, r)
                to_y(1, d, h, 0, far, r)
            to_sibling(0, d, h, 0, r)

    def passed_on(step, d, k):
        if d in (1, 3):
            return (2,) if k == 1 else ()
        return () if k != 2 else (3, 4) if last_leg(step, d) else (3,)

    def last_leg(step, d):
        return step == (0 if d in (0, 1) else 1)

    def from_y(k, *ds):
        for d in ds:
            for h in range(PARTS):
                steps = [step for step in range(2) if k < YN // 2 or last_leg(step, d)]
                arrived(x.at[pl.ds(0, PART * len(steps))], y_recv.at[k - 1, d, h])
                for step in steps:
                    r = source(step, d, k)
                    for far in passed_on(step, d, k):
                        to_y(step, d, h, k, far, r)
                    if d == 0 and k > 2:
                        for o in (1, 3):
                            to_z(o, h, r, y_recv.at[k - 1, ZN - o, h])
                    to_sibling(step, d, h, k, r)

    from_y(1, 0)
    from_y(2, 0)
    arrived(ra.at[pl.ds(0, YN - 1)], g_recv.at[0])
    part[...] = jnp.sum(ra[...], axis=0)
    rb[w] = part[...]
    for o in range(1, WN):
        send(part, rb.at[w], sent.at[6], g_recv.at[1], at_row(w_row(o)))

    from_z(1)
    from_z(3)

    from_y(3, 0)
    from_z(2)
    from_y(1, 1, 3)
    arrived(rb.at[pl.ds(0, WN - 1)], g_recv.at[1])
    final[y] = jnp.sum(rb[...], axis=0)
    for o in range(1, YN):
        send(final.at[y], final.at[y], sent.at[7], g_recv.at[2], at_row(y_row(o)))

    from_y(4, 0)
    from_y(1, 2)
    from_y(2, 2)

    from_y(2, 1, 3)
    from_y(3, 1, 3)
    from_y(4, 1, 3)
    from_y(3, 2)
    from_y(4, 2)

    arrived(final.at[pl.ds(0, YN - 1)], g_recv.at[2])
    for q in range(YN):
        wg_out[(q // 2) * 8:(q // 2) * 8 + 8, (q % 2) * TILE:(q % 2 + 1) * TILE] = final[q]

    arrived(x.at[pl.ds(0, BLOCKS * ROWS // CORES)], s_recv.at[0])

    for load in loads[4:]:
        load.wait()
    in_use = count[0]
    first = row * BLOCKS
    group = 11
    total = jnp.zeros((BLOCKS * FEAT, TILE), jnp.float32)
    for g in range(0, SLOTS, group):
        pieces = []
        for t in range(g, g + group):
            here = x[coords[0, t]]
            j = jnp.where(t < in_use, coords[1, t] - first, -1)
            zero = jnp.zeros_like(here)
            pieces.append(jnp.concatenate(
                [jnp.where(j == b, here, zero) for b in range(BLOCKS)], axis=0))
        total += jnp.dot(
            jnp.concatenate(pieces, axis=1),
            tiles[g:g + group].reshape(group * TILE, TILE),
            preferred_element_type=jnp.float32,
        )
    for b in range(BLOCKS):
        fg_out[:, b * TILE:(b + 1) * TILE] = total[b * FEAT:(b + 1) * FEAT].astype(jnp.bfloat16)

    for n, ref in enumerate((
        wpart.at[pl.ds(0, others)], masked.at[pl.ds(0, PARTS * others)],
        x.at[pl.ds(0, len(z_sends) * PART)], x.at[pl.ds(0, len(y_sends) * PART)],
        x.at[pl.ds(0, BLOCKS * ROWS // CORES)],
        wl.at[pl.ds(0, YN - 1)], rb.at[pl.ds(0, WN - 1)], final.at[pl.ds(0, YN - 1)],
    )):
        arrived(ref, sent.at[n])


def shards(grad_out, pre_act, aggregated, weight, tiles, tile_coords, tile_count):
    bf16, f32 = jnp.bfloat16, jnp.float32
    vmem, dma = pltpu.VMEM, pltpu.SemaphoreType.DMA
    return pl.pallas_call(
        kernel,
        out_shape=(
            vmem((FEAT, NODES), bf16),
            vmem((FEAT, COLS * FEAT), f32),
        ),
        in_specs=[pl.BlockSpec(memory_space=pl.ANY)] * 7,
        out_specs=(pl.BlockSpec(memory_space=vmem), pl.BlockSpec(memory_space=vmem)),
        scratch_shapes=[
            vmem((FEAT, NODES), bf16),
            vmem((FEAT, NODES), bf16),
            vmem((FEAT, NODES), bf16),
            vmem((FEAT, COLS * FEAT), bf16),
            vmem((SLOTS, TILE, TILE), bf16),
            pltpu.SMEM((2, SLOTS), jnp.int32),
            pltpu.SMEM((1,), jnp.int32),
            vmem((PARTS * COLS, FEAT, PNODES), bf16),
            vmem((COLS, FEAT, TILE), bf16),
            vmem((TILE, COLS * FEAT), f32),
            vmem((ROWS * BLOCKS, FEAT, TILE), bf16),
            vmem((YN, 8, TILE), f32),
            vmem((YN, 8, TILE), f32),
            vmem((8, TILE), f32),
            vmem((WN, 8, TILE), f32),
            vmem((YN, 8, TILE), f32),
            dma((7,)),
            dma((8,)), dma((1,)), dma((PARTS,)), dma((ZN, PARTS)), dma((YN // 2, ZN, PARTS)), dma((1,)), dma((3,)),
        ],
        compiler_params=pltpu.CompilerParams(
            collective_id=0, has_side_effects=True, vmem_limit_bytes=55168 * 1024,
        ),
        cost_estimate=pl.CostEstimate(flops=300_000_000, bytes_accessed=6_000_000, transcendentals=0),
    )(grad_out, pre_act, aggregated, weight.T, tiles, tile_coords.T, tile_count)


def solution(mesh):
    in_specs = (
        P("col", "row"),
        P("col", "row"),
        P("col", "row"),
        P(None, "col"),
        P("row", None, None),
        P("row", None),
        P("row"),
    )
    out_specs = (P("col", "row"), P("col", None))
    return jax.shard_map(shards, mesh=mesh, in_specs=in_specs, out_specs=out_specs, check_vma=False)
```

```python
import jax
import jax.numpy as jnp
from jax import lax
from jax.experimental import pallas as pl
from jax.experimental.pallas import tpu as pltpu
from jax.sharding import PartitionSpec as P

YN, ZN, CORES, COLS = 8, 4, 2, 8
WN = ZN * CORES
ROWS = YN * WN
TILE = 128
BLOCKS = 4
FEAT = 32
NODES = BLOCKS * TILE
PARTS = 1
PART = BLOCKS // PARTS
PNODES = PART * TILE
SLOTS = 99
MESH = pl.DeviceIdType.MESH
SHEET = ((1, 2), (1, 1), (1, 3), (1, 0), (0, 2), (0, 1), (0, 3))


def kernel(
    go_hbm, pa_hbm, agg_hbm, wt_hbm, tiles_hbm, coords_hbm, count_hbm,
    fg_out, wg_out,
    go, pa, agg, wt, tiles, coords, count,
    masked, wpart, wrow, x, wl, ra, part, rb, final,
    in_sem, sent, w_recv, m_recv, z_recv, y_recv, s_recv, g_recv,
):
    row = lax.axis_index("row")
    col = lax.axis_index("col")
    y = row // WN
    w = row % WN
    z = w // CORES
    core = w % CORES
    sibling = row + 1 - 2 * core

    def col_of(dz, dx):
        return ((col // 4 + dz) % 2) * 4 + (col + dx) % 4

    def at_col(c):
        return {"row": row, "col": c}

    def at_row(r):
        return {"row": r, "col": col}

    def y_row(o):
        return ((y + o) % YN) * WN + w

    def w_row(o):
        return y * WN + (w + o) % WN

    def z_row(o):
        return y * WN + ((z + o) % ZN) * CORES + core

    loads = [
        pltpu.make_async_copy(src, dst, in_sem.at[n])
        for n, (src, dst) in enumerate((
            (go_hbm, go), (pa_hbm, pa), (wt_hbm, wt), (agg_hbm, agg),
            (coords_hbm, coords), (count_hbm, count), (tiles_hbm, tiles),
        ))
    ]
    for load in loads:
        load.start()

    barrier = pltpu.get_barrier_semaphore()
    for dz, dx in SHEET:
        pl.semaphore_signal(barrier, inc=1, device_id=at_col(col_of(dz, dx)), device_id_type=MESH)
    for o in range(1, YN):
        pl.semaphore_signal(barrier, inc=1, device_id=at_row(y_row(o)), device_id_type=MESH)
    for o in range(1, WN):
        pl.semaphore_signal(barrier, inc=1, device_id=at_row(w_row(o)), device_id_type=MESH)

    loads[0].wait()
    loads[1].wait()
    for h in range(PARTS):
        own_nodes = slice(h * PNODES, (h + 1) * PNODES)
        g = go[:, own_nodes]
        masked[h * COLS + col] = jnp.where(pa[:, own_nodes] > 0, g, jnp.zeros_like(g))
    loads[2].wait()
    wpart[col] = wt[:, pl.ds(pl.multiple_of((col // 4) * TILE, TILE), TILE)]

    pl.semaphore_wait(barrier, COLS - 1 + YN - 1 + WN - 1)

    def remote(src, dst, send, recv, to):
        return pltpu.make_async_remote_copy(
            src_ref=src, dst_ref=dst, send_sem=send, recv_sem=recv,
            device_id=to, device_id_type=MESH,
        )

    def send(src, dst, send_sem, recv_sem, to):
        remote(src, dst, send_sem, recv_sem, to).start()

    def arrived(ref, sem):
        pltpu.make_async_copy(ref, ref, sem).wait()

    y_sends, z_sends = [], []

    others = COLS - 1
    for dz, dx in SHEET:
        peer = col_of(dz, dx)
        send(
            wt.at[:, pl.ds(pl.multiple_of((peer // 4) * TILE, TILE), TILE)],
            wpart.at[col], sent.at[0], w_recv.at[0], at_col(peer),
        )
    for h in range(PARTS):
        for dz, dx in SHEET:
            send(masked.at[h * COLS + col], masked.at[h * COLS + col], sent.at[1], m_recv.at[h],
                 at_col(col_of(dz, dx)))
    arrived(wpart.at[pl.ds(0, others)], w_recv.at[0])
    wrow[...] = wpart[...].reshape(COLS * FEAT, TILE).astype(jnp.float32).T
    own_w = wrow[pl.ds(pl.multiple_of((col % 4) * FEAT, FEAT), FEAT), :].astype(jnp.bfloat16)
    def part_of(r, h):
        return x.at[pl.ds(r * BLOCKS + h * PART, PART)]

    def to_y(step, d, h, k, far, r):
        send(part_of(r, h), part_of(r, h), sent.at[3], y_recv.at[far - 1, d, h],
             at_row(y_row((1 - 2 * step) * (far - k))))
        y_sends.append(far)

    def to_z(d, h, r, sem):
        send(part_of(r, h), part_of(r, h), sent.at[2], sem, at_row(z_row(d)))
        z_sends.append(d)

    def to_sibling(step, d, h, k, r):
        send(part_of(r, h), part_of(r, h), sent.at[4], s_recv.at[0], at_row(sibling))

    def source(step, d, k):
        return ((y - (1 - 2 * step) * k) % YN) * WN + ((z + d) % ZN) * CORES + core

    def masked_part(h):
        return masked[h * COLS:(h + 1) * COLS].reshape(COLS * FEAT, PNODES)

    for h in range(PARTS):
        arrived(masked.at[pl.ds(0, others)], m_recv.at[h])
        node_grad = jnp.dot(
            own_w, masked_part(h), preferred_element_type=jnp.float32
        ).astype(jnp.bfloat16)
        for b in range(PART):
            x[row * BLOCKS + h * PART + b] = node_grad[:, b * TILE:(b + 1) * TILE]
        for far in (1, 2):
            for step in range(2):
                to_y(step, 0, h, 0, far, row)
        for d in (2, 1, 3):
            to_z(d, h, row, z_recv.at[ZN - d, h])
        to_sibling(0, 0, h, 0, row)

    loads[3].wait()
    wgrad = sum(
        lax.dot_general(
            agg[:, h * PNODES:(h + 1) * PNODES], masked_part(h),
            (((1,), (1,)), ((), ())), preferred_element_type=jnp.float32,
        )
        for h in range(PARTS)
    )
    for q in range(YN):
        piece = wgrad[(q // 2) * 8:(q // 2) * 8 + 8, (q % 2) * TILE:(q % 2 + 1) * TILE]
        wl[q] = piece
    ra[y] = wl[y]
    for o in range(1, YN):
        send(wl.at[(y + o) % YN], ra.at[y], sent.at[5], g_recv.at[0], at_row(y_row(o)))

    def from_z(d):
        r = z_row(d)
        for h in range(PARTS):
            arrived(part_of(r, h), z_recv.at[d, h])
            for far in (1, 2) if d == 2 else (1,):
                to_y(0, d, h, 0, far, r)
                to_y(1, d, h, 0, far, r)
            to_sibling(0, d, h, 0, r)

    def passed_on(step, d, k):
        if d in (1, 3):
            return (2,) if k == 1 else ()
        return () if k != 2 else (3, 4) if last_leg(step, d) else (3,)

    def last_leg(step, d):
        return step == (0 if d in (0, 1) else 1)

    def from_y(k, *ds):
        for d in ds:
            for h in range(PARTS):
                steps = [step for step in range(2) if k < YN // 2 or last_leg(step, d)]
                arrived(x.at[pl.ds(0, PART * len(steps))], y_recv.at[k - 1, d, h])
                for step in steps:
                    r = source(step, d, k)
                    for far in passed_on(step, d, k):
                        to_y(step, d, h, k, far, r)
                    if d == 0 and k > 2:
                        for o in (1, 3):
                            to_z(o, h, r, y_recv.at[k - 1, ZN - o, h])
                    to_sibling(step, d, h, k, r)

    from_y(1, 0)
    from_y(2, 0)
    arrived(ra.at[pl.ds(0, YN - 1)], g_recv.at[0])
    part[...] = jnp.sum(ra[...], axis=0)
    rb[w] = part[...]
    for o in range(1, WN):
        send(part, rb.at[w], sent.at[6], g_recv.at[1], at_row(w_row(o)))

    from_z(1)
    from_z(3)

    from_z(2)
    from_y(3, 0)
    from_y(1, 1, 3)
    arrived(rb.at[pl.ds(0, WN - 1)], g_recv.at[1])
    final[y] = jnp.sum(rb[...], axis=0)
    for o in range(1, YN):
        send(final.at[y], final.at[y], sent.at[7], g_recv.at[2], at_row(y_row(o)))

    from_y(4, 0)
    from_y(1, 2)
    from_y(2, 2)

    from_y(2, 1, 3)
    from_y(3, 1, 3)
    from_y(4, 1, 3)
    from_y(3, 2)
    from_y(4, 2)

    arrived(final.at[pl.ds(0, YN - 1)], g_recv.at[2])
    for q in range(YN):
        wg_out[(q // 2) * 8:(q // 2) * 8 + 8, (q % 2) * TILE:(q % 2 + 1) * TILE] = final[q]

    arrived(x.at[pl.ds(0, BLOCKS * ROWS // CORES)], s_recv.at[0])

    for load in loads[4:]:
        load.wait()
    in_use = count[0]
    first = row * BLOCKS
    group = 11
    total = jnp.zeros((BLOCKS * FEAT, TILE), jnp.float32)
    for g in range(0, SLOTS, group):
        pieces = []
        for t in range(g, g + group):
            here = x[coords[0, t]]
            j = jnp.where(t < in_use, coords[1, t] - first, -1)
            zero = jnp.zeros_like(here)
            pieces.append(jnp.concatenate(
                [jnp.where(j == b, here, zero) for b in range(BLOCKS)], axis=0))
        total += jnp.dot(
            jnp.concatenate(pieces, axis=1),
            tiles[g:g + group].reshape(group * TILE, TILE),
            preferred_element_type=jnp.float32,
        )
    for b in range(BLOCKS):
        fg_out[:, b * TILE:(b + 1) * TILE] = total[b * FEAT:(b + 1) * FEAT].astype(jnp.bfloat16)

    for n, ref in enumerate((
        wpart.at[pl.ds(0, others)], masked.at[pl.ds(0, PARTS * others)],
        x.at[pl.ds(0, len(z_sends) * PART)], x.at[pl.ds(0, len(y_sends) * PART)],
        x.at[pl.ds(0, BLOCKS * ROWS // CORES)],
        wl.at[pl.ds(0, YN - 1)], rb.at[pl.ds(0, WN - 1)], final.at[pl.ds(0, YN - 1)],
    )):
        arrived(ref, sent.at[n])


def shards(grad_out, pre_act, aggregated, weight, tiles, tile_coords, tile_count):
    bf16, f32 = jnp.bfloat16, jnp.float32
    vmem, dma = pltpu.VMEM, pltpu.SemaphoreType.DMA
    return pl.pallas_call(
        kernel,
        out_shape=(
            vmem((FEAT, NODES), bf16),
            vmem((FEAT, COLS * FEAT), f32),
        ),
        in_specs=[pl.BlockSpec(memory_space=pl.ANY)] * 7,
        out_specs=(pl.BlockSpec(memory_space=vmem), pl.BlockSpec(memory_space=vmem)),
        scratch_shapes=[
            vmem((FEAT, NODES), bf16),
            vmem((FEAT, NODES), bf16),
            vmem((FEAT, NODES), bf16),
            vmem((FEAT, COLS * FEAT), bf16),
            vmem((SLOTS, TILE, TILE), bf16),
            pltpu.SMEM((2, SLOTS), jnp.int32),
            pltpu.SMEM((1,), jnp.int32),
            vmem((PARTS * COLS, FEAT, PNODES), bf16),
            vmem((COLS, FEAT, TILE), bf16),
            vmem((TILE, COLS * FEAT), f32),
            vmem((ROWS * BLOCKS, FEAT, TILE), bf16),
            vmem((YN, 8, TILE), f32),
            vmem((YN, 8, TILE), f32),
            vmem((8, TILE), f32),
            vmem((WN, 8, TILE), f32),
            vmem((YN, 8, TILE), f32),
            dma((7,)),
            dma((8,)), dma((1,)), dma((PARTS,)), dma((ZN, PARTS)), dma((YN // 2, ZN, PARTS)), dma((1,)), dma((3,)),
        ],
        compiler_params=pltpu.CompilerParams(
            collective_id=0, has_side_effects=True, vmem_limit_bytes=55168 * 1024,
        ),
        cost_estimate=pl.CostEstimate(flops=300_000_000, bytes_accessed=6_000_000, transcendentals=0),
    )(grad_out, pre_act, aggregated, weight.T, tiles, tile_coords.T, tile_count)


def solution(mesh):
    in_specs = (
        P("col", "row"),
        P("col", "row"),
        P("col", "row"),
        P(None, "col"),
        P("row", None, None),
        P("row", None),
        P("row"),
    )
    out_specs = (P("col", "row"), P("col", None))
    return jax.shard_map(shards, mesh=mesh, in_specs=in_specs, out_specs=out_specs, check_vma=False)
```

```python
import jax
import jax.numpy as jnp
from jax import lax
from jax.experimental import pallas as pl
from jax.experimental.pallas import tpu as pltpu
from jax.sharding import PartitionSpec as P

YN, ZN, CORES, COLS = 8, 4, 2, 8
WN = ZN * CORES
ROWS = YN * WN
TILE = 128
BLOCKS = 4
FEAT = 32
NODES = BLOCKS * TILE
PARTS = 1
PART = BLOCKS // PARTS
PNODES = PART * TILE
SLOTS = 99
MESH = pl.DeviceIdType.MESH
SHEET = ((1, 2), (1, 1), (1, 3), (1, 0), (0, 2), (0, 1), (0, 3))


def kernel(
    go_hbm, pa_hbm, agg_hbm, wt_hbm, tiles_hbm, coords_hbm, count_hbm,
    fg_out, wg_out,
    go, pa, agg, wt, tiles, coords, count,
    masked, wpart, wrow, x, wl, ra, part, rb, final,
    in_sem, sent, w_recv, m_recv, z_recv, y_recv, s_recv, g_recv,
):
    row = lax.axis_index("row")
    col = lax.axis_index("col")
    y = row // WN
    w = row % WN
    z = w // CORES
    core = w % CORES
    sibling = row + 1 - 2 * core

    def col_of(dz, dx):
        return ((col // 4 + dz) % 2) * 4 + (col + dx) % 4

    def at_col(c):
        return {"row": row, "col": c}

    def at_row(r):
        return {"row": r, "col": col}

    def y_row(o):
        return ((y + o) % YN) * WN + w

    def w_row(o):
        return y * WN + (w + o) % WN

    def z_row(o):
        return y * WN + ((z + o) % ZN) * CORES + core

    loads = [
        pltpu.make_async_copy(src, dst, in_sem.at[n])
        for n, (src, dst) in enumerate((
            (go_hbm, go), (pa_hbm, pa), (wt_hbm, wt), (agg_hbm, agg),
            (coords_hbm, coords), (count_hbm, count), (tiles_hbm, tiles),
        ))
    ]
    for load in loads:
        load.start()

    barrier = pltpu.get_barrier_semaphore()
    for dz, dx in SHEET:
        pl.semaphore_signal(barrier, inc=1, device_id=at_col(col_of(dz, dx)), device_id_type=MESH)
    for o in range(1, YN):
        pl.semaphore_signal(barrier, inc=1, device_id=at_row(y_row(o)), device_id_type=MESH)
    for o in range(1, WN):
        pl.semaphore_signal(barrier, inc=1, device_id=at_row(w_row(o)), device_id_type=MESH)

    loads[0].wait()
    loads[1].wait()
    for h in range(PARTS):
        own_nodes = slice(h * PNODES, (h + 1) * PNODES)
        g = go[:, own_nodes]
        masked[h * COLS + col] = jnp.where(pa[:, own_nodes] > 0, g, jnp.zeros_like(g))
    loads[2].wait()
    wpart[col] = wt[:, pl.ds(pl.multiple_of((col // 4) * TILE, TILE), TILE)]

    pl.semaphore_wait(barrier, COLS - 1 + YN - 1 + WN - 1)

    def remote(src, dst, send, recv, to):
        return pltpu.make_async_remote_copy(
            src_ref=src, dst_ref=dst, send_sem=send, recv_sem=recv,
            device_id=to, device_id_type=MESH,
        )

    def send(src, dst, send_sem, recv_sem, to):
        remote(src, dst, send_sem, recv_sem, to).start()

    def arrived(ref, sem):
        pltpu.make_async_copy(ref, ref, sem).wait()

    y_sends, z_sends = [], []

    others = COLS - 1
    for dz, dx in SHEET:
        peer = col_of(dz, dx)
        send(
            wt.at[:, pl.ds(pl.multiple_of((peer // 4) * TILE, TILE), TILE)],
            wpart.at[col], sent.at[0], w_recv.at[0], at_col(peer),
        )
    for h in range(PARTS):
        for dz, dx in SHEET:
            send(masked.at[h * COLS + col], masked.at[h * COLS + col], sent.at[1], m_recv.at[h],
                 at_col(col_of(dz, dx)))
    arrived(wpart.at[pl.ds(0, others)], w_recv.at[0])
    wrow[...] = wpart[...].reshape(COLS * FEAT, TILE).astype(jnp.float32).T
    own_w = wrow[pl.ds(pl.multiple_of((col % 4) * FEAT, FEAT), FEAT), :].astype(jnp.bfloat16)
    def part_of(r, h):
        return x.at[pl.ds(r * BLOCKS + h * PART, PART)]

    def to_y(step, d, h, k, far, r):
        send(part_of(r, h), part_of(r, h), sent.at[3], y_recv.at[far - 1, d, h],
             at_row(y_row((1 - 2 * step) * (far - k))))
        y_sends.append(far)

    def to_z(d, h, r, sem):
        send(part_of(r, h), part_of(r, h), sent.at[2], sem, at_row(z_row(d)))
        z_sends.append(d)

    def to_sibling(step, d, h, k, r):
        send(part_of(r, h), part_of(r, h), sent.at[4], s_recv.at[0], at_row(sibling))

    def source(step, d, k):
        return ((y - (1 - 2 * step) * k) % YN) * WN + ((z + d) % ZN) * CORES + core

    def masked_part(h):
        return masked[h * COLS:(h + 1) * COLS].reshape(COLS * FEAT, PNODES)

    for h in range(PARTS):
        arrived(masked.at[pl.ds(0, others)], m_recv.at[h])
        node_grad = jnp.dot(
            own_w, masked_part(h), preferred_element_type=jnp.float32
        ).astype(jnp.bfloat16)
        for b in range(PART):
            x[row * BLOCKS + h * PART + b] = node_grad[:, b * TILE:(b + 1) * TILE]
        for far in (1, 2):
            for step in range(2):
                to_y(step, 0, h, 0, far, row)
        for d in (2, 1, 3):
            to_z(d, h, row, z_recv.at[ZN - d, h])
        to_sibling(0, 0, h, 0, row)

    loads[3].wait()
    wgrad = sum(
        lax.dot_general(
            agg[:, h * PNODES:(h + 1) * PNODES], masked_part(h),
            (((1,), (1,)), ((), ())), preferred_element_type=jnp.float32,
        )
        for h in range(PARTS)
    )
    for q in range(YN):
        piece = wgrad[(q // 2) * 8:(q // 2) * 8 + 8, (q % 2) * TILE:(q % 2 + 1) * TILE]
        wl[q] = piece
    ra[y] = wl[y]
    for o in range(1, YN):
        send(wl.at[(y + o) % YN], ra.at[y], sent.at[5], g_recv.at[0], at_row(y_row(o)))

    def from_z(d):
        r = z_row(d)
        for h in range(PARTS):
            arrived(part_of(r, h), z_recv.at[d, h])
            for far in (1, 2) if d == 2 else (1,):
                to_y(0, d, h, 0, far, r)
                to_y(1, d, h, 0, far, r)
            to_sibling(0, d, h, 0, r)

    def passed_on(step, d, k):
        if d in (1, 3):
            return (2,) if k == 1 else ()
        return () if k != 2 else (3, 4) if last_leg(step, d) else (3,)

    def last_leg(step, d):
        return step == (0 if d in (0, 1) else 1)

    def from_y(k, *ds):
        for d in ds:
            for h in range(PARTS):
                steps = [step for step in range(2) if k < YN // 2 or last_leg(step, d)]
                arrived(x.at[pl.ds(0, PART * len(steps))], y_recv.at[k - 1, d, h])
                for step in steps:
                    r = source(step, d, k)
                    for far in passed_on(step, d, k):
                        to_y(step, d, h, k, far, r)
                    if d == 0 and k > 2:
                        for o in (1, 3):
                            to_z(o, h, r, y_recv.at[k - 1, ZN - o, h])
                    to_sibling(step, d, h, k, r)

    from_y(1, 0)
    from_y(2, 0)
    arrived(ra.at[pl.ds(0, YN - 1)], g_recv.at[0])
    part[...] = jnp.sum(ra[...], axis=0)
    rb[w] = part[...]
    for o in range(1, WN):
        send(part, rb.at[w], sent.at[6], g_recv.at[1], at_row(w_row(o)))

    from_z(1)
    from_z(3)

    from_y(3, 0)
    from_z(2)
    from_y(1, 1, 3)
    arrived(rb.at[pl.ds(0, WN - 1)], g_recv.at[1])
    final[y] = jnp.sum(rb[...], axis=0)
    for o in range(1, YN):
        send(final.at[y], final.at[y], sent.at[7], g_recv.at[2], at_row(y_row(o)))

    from_y(4, 0)
    from_y(1, 2)
    from_y(2, 2)

    from_y(2, 1, 3)
    from_y(3, 1, 3)
    from_y(4, 1, 3)
    from_y(3, 2)
    from_y(4, 2)

    arrived(final.at[pl.ds(0, YN - 1)], g_recv.at[2])
    for q in range(YN):
        wg_out[(q // 2) * 8:(q // 2) * 8 + 8, (q % 2) * TILE:(q % 2 + 1) * TILE] = final[q]

    arrived(x.at[pl.ds(0, BLOCKS * ROWS // CORES)], s_recv.at[0])

    for load in loads[4:]:
        load.wait()
    in_use = count[0]
    first = row * BLOCKS
    group = 11
    total = jnp.zeros((BLOCKS * FEAT, TILE), jnp.float32)
    for g in range(0, SLOTS, group):
        pieces = []
        for t in range(g, g + group):
            here = x[coords[0, t]]
            j = jnp.where(t < in_use, coords[1, t] - first, -1)
            zero = jnp.zeros_like(here)
            pieces.append(jnp.concatenate(
                [jnp.where(j == b, here, zero) for b in range(BLOCKS)], axis=0))
        total += jnp.dot(
            jnp.concatenate(pieces, axis=1),
            tiles[g:g + group].reshape(group * TILE, TILE),
            preferred_element_type=jnp.float32,
        )
    for b in range(BLOCKS):
        fg_out[:, b * TILE:(b + 1) * TILE] = total[b * FEAT:(b + 1) * FEAT].astype(jnp.bfloat16)

    for n, ref in enumerate((
        wpart.at[pl.ds(0, others)], masked.at[pl.ds(0, PARTS * others)],
        x.at[pl.ds(0, len(z_sends) * PART)], x.at[pl.ds(0, len(y_sends) * PART)],
        x.at[pl.ds(0, BLOCKS * ROWS // CORES)],
        wl.at[pl.ds(0, YN - 1)], rb.at[pl.ds(0, WN - 1)], final.at[pl.ds(0, YN - 1)],
    )):
        arrived(ref, sent.at[n])


def shards(grad_out, pre_act, aggregated, weight, tiles, tile_coords, tile_count):
    bf16, f32 = jnp.bfloat16, jnp.float32
    vmem, dma = pltpu.VMEM, pltpu.SemaphoreType.DMA
    return pl.pallas_call(
        kernel,
        out_shape=(
            vmem((FEAT, NODES), bf16),
            vmem((FEAT, COLS * FEAT), f32),
        ),
        in_specs=[pl.BlockSpec(memory_space=pl.ANY)] * 7,
        out_specs=(pl.BlockSpec(memory_space=vmem), pl.BlockSpec(memory_space=vmem)),
        scratch_shapes=[
            vmem((FEAT, NODES), bf16),
            vmem((FEAT, NODES), bf16),
            vmem((FEAT, NODES), bf16),
            vmem((FEAT, COLS * FEAT), bf16),
            vmem((SLOTS, TILE, TILE), bf16),
            pltpu.SMEM((2, SLOTS), jnp.int32),
            pltpu.SMEM((1,), jnp.int32),
            vmem((PARTS * COLS, FEAT, PNODES), bf16),
            vmem((COLS, FEAT, TILE), bf16),
            vmem((TILE, COLS * FEAT), f32),
            vmem((ROWS * BLOCKS, FEAT, TILE), bf16),
            vmem((YN, 8, TILE), f32),
            vmem((YN, 8, TILE), f32),
            vmem((8, TILE), f32),
            vmem((WN, 8, TILE), f32),
            vmem((YN, 8, TILE), f32),
            dma((7,)),
            dma((8,)), dma((1,)), dma((PARTS,)), dma((ZN, PARTS)), dma((YN // 2, ZN, PARTS)), dma((1,)), dma((3,)),
        ],
        compiler_params=pltpu.CompilerParams(
            collective_id=0, has_side_effects=True, vmem_limit_bytes=55168 * 1024,
        ),
        cost_estimate=pl.CostEstimate(flops=300_000_000, bytes_accessed=6_000_000, transcendentals=0),
    )(grad_out, pre_act, aggregated, weight.T, tiles, tile_coords.T, tile_count)


def solution(mesh):
    in_specs = (
        P("col", "row"),
        P("col", "row"),
        P("col", "row"),
        P(None, "col"),
        P("row", None, None),
        P("row", None),
        P("row"),
    )
    out_specs = (P("col", "row"), P("col", None))
    return jax.shard_map(shards, mesh=mesh, in_specs=in_specs, out_specs=out_specs, check_vma=False)
```

```python
import jax
import jax.numpy as jnp
from jax import lax
from jax.experimental import pallas as pl
from jax.experimental.pallas import tpu as pltpu
from jax.sharding import PartitionSpec as P

YN, ZN, CORES, COLS = 8, 4, 2, 8
WN = ZN * CORES
ROWS = YN * WN
TILE = 128
BLOCKS = 4
FEAT = 32
NODES = BLOCKS * TILE
PARTS = 1
PART = BLOCKS // PARTS
PNODES = PART * TILE
SLOTS = 99
MESH = pl.DeviceIdType.MESH
SHEET = ((1, 2), (1, 1), (1, 3), (1, 0), (0, 2), (0, 1), (0, 3))


def kernel(
    go_hbm, pa_hbm, agg_hbm, wt_hbm, tiles_hbm, coords_hbm, count_hbm,
    fg_out, wg_out,
    go, pa, agg, wt, tiles, coords, count,
    masked, wpart, wrow, x, wl, ra, part, rb, final,
    in_sem, sent, w_recv, m_recv, z_recv, y_recv, s_recv, g_recv,
):
    row = lax.axis_index("row")
    col = lax.axis_index("col")
    y = row // WN
    w = row % WN
    z = w // CORES
    core = w % CORES
    sibling = row + 1 - 2 * core

    def col_of(dz, dx):
        return ((col // 4 + dz) % 2) * 4 + (col + dx) % 4

    def at_col(c):
        return {"row": row, "col": c}

    def at_row(r):
        return {"row": r, "col": col}

    def y_row(o):
        return ((y + o) % YN) * WN + w

    def w_row(o):
        return y * WN + (w + o) % WN

    def z_row(o):
        return y * WN + ((z + o) % ZN) * CORES + core

    loads = [
        pltpu.make_async_copy(src, dst, in_sem.at[n])
        for n, (src, dst) in enumerate((
            (go_hbm, go), (pa_hbm, pa), (wt_hbm, wt), (agg_hbm, agg),
            (coords_hbm, coords), (count_hbm, count), (tiles_hbm, tiles),
        ))
    ]
    for load in loads:
        load.start()

    barrier = pltpu.get_barrier_semaphore()
    for dz, dx in SHEET:
        pl.semaphore_signal(barrier, inc=1, device_id=at_col(col_of(dz, dx)), device_id_type=MESH)
    for o in range(1, YN):
        pl.semaphore_signal(barrier, inc=1, device_id=at_row(y_row(o)), device_id_type=MESH)
    for o in range(1, WN):
        pl.semaphore_signal(barrier, inc=1, device_id=at_row(w_row(o)), device_id_type=MESH)

    loads[0].wait()
    loads[1].wait()
    for h in range(PARTS):
        own_nodes = slice(h * PNODES, (h + 1) * PNODES)
        g = go[:, own_nodes]
        masked[h * COLS + col] = jnp.where(pa[:, own_nodes] > 0, g, jnp.zeros_like(g))
    loads[2].wait()
    wpart[col] = wt[:, pl.ds(pl.multiple_of((col // 4) * TILE, TILE), TILE)]

    pl.semaphore_wait(barrier, COLS - 1 + YN - 1 + WN - 1)

    def remote(src, dst, send, recv, to):
        return pltpu.make_async_remote_copy(
            src_ref=src, dst_ref=dst, send_sem=send, recv_sem=recv,
            device_id=to, device_id_type=MESH,
        )

    def send(src, dst, send_sem, recv_sem, to):
        remote(src, dst, send_sem, recv_sem, to).start()

    def arrived(ref, sem):
        pltpu.make_async_copy(ref, ref, sem).wait()

    y_sends, z_sends = [], []

    others = COLS - 1
    for dz, dx in SHEET:
        peer = col_of(dz, dx)
        send(
            wt.at[:, pl.ds(pl.multiple_of((peer // 4) * TILE, TILE), TILE)],
            wpart.at[col], sent.at[0], w_recv.at[0], at_col(peer),
        )
    for h in range(PARTS):
        for dz, dx in SHEET:
            send(masked.at[h * COLS + col], masked.at[h * COLS + col], sent.at[1], m_recv.at[h],
                 at_col(col_of(dz, dx)))
    arrived(wpart.at[pl.ds(0, others)], w_recv.at[0])
    wrow[...] = wpart[...].reshape(COLS * FEAT, TILE).astype(jnp.float32).T
    own_w = wrow[pl.ds(pl.multiple_of((col % 4) * FEAT, FEAT), FEAT), :].astype(jnp.bfloat16)
    def part_of(r, h):
        return x.at[pl.ds(r * BLOCKS + h * PART, PART)]

    def to_y(step, d, h, k, far, r):
        send(part_of(r, h), part_of(r, h), sent.at[3], y_recv.at[far - 1, d, h],
             at_row(y_row((1 - 2 * step) * (far - k))))
        y_sends.append(far)

    def to_z(d, h, r, sem):
        send(part_of(r, h), part_of(r, h), sent.at[2], sem, at_row(z_row(d)))
        z_sends.append(d)

    def to_sibling(step, d, h, k, r):
        send(part_of(r, h), part_of(r, h), sent.at[4], s_recv.at[0], at_row(sibling))

    def source(step, d, k):
        return ((y - (1 - 2 * step) * k) % YN) * WN + ((z + d) % ZN) * CORES + core

    def masked_part(h):
        return masked[h * COLS:(h + 1) * COLS].reshape(COLS * FEAT, PNODES)

    for h in range(PARTS):
        arrived(masked.at[pl.ds(0, others)], m_recv.at[h])
        node_grad = jnp.dot(
            own_w, masked_part(h), preferred_element_type=jnp.float32
        ).astype(jnp.bfloat16)
        for b in range(PART):
            x[row * BLOCKS + h * PART + b] = node_grad[:, b * TILE:(b + 1) * TILE]
        for far in (1, 2):
            for step in range(2):
                to_y(step, 0, h, 0, far, row)
        for d in (1, 3, 2):
            to_z(d, h, row, z_recv.at[ZN - d, h])
        to_sibling(0, 0, h, 0, row)

    loads[3].wait()
    wgrad = sum(
        lax.dot_general(
            agg[:, h * PNODES:(h + 1) * PNODES], masked_part(h),
            (((1,), (1,)), ((), ())), preferred_element_type=jnp.float32,
        )
        for h in range(PARTS)
    )
    for q in range(YN):
        piece = wgrad[(q // 2) * 8:(q // 2) * 8 + 8, (q % 2) * TILE:(q % 2 + 1) * TILE]
        wl[q] = piece
    ra[y] = wl[y]
    for o in range(1, YN):
        send(wl.at[(y + o) % YN], ra.at[y], sent.at[5], g_recv.at[0], at_row(y_row(o)))

    def from_z(d):
        r = z_row(d)
        for h in range(PARTS):
            arrived(part_of(r, h), z_recv.at[d, h])
            for far in (1, 2) if d == 2 else (1,):
                to_y(0, d, h, 0, far, r)
                to_y(1, d, h, 0, far, r)
            to_sibling(0, d, h, 0, r)

    def passed_on(step, d, k):
        if d in (1, 3):
            return (2,) if k == 1 else ()
        return () if k != 2 else (3, 4) if last_leg(step, d) else (3,)

    def last_leg(step, d):
        return step == (0 if d in (0, 1) else 1)

    def from_y(k, *ds):
        for d in ds:
            for h in range(PARTS):
                steps = [step for step in range(2) if k < YN // 2 or last_leg(step, d)]
                arrived(x.at[pl.ds(0, PART * len(steps))], y_recv.at[k - 1, d, h])
                for step in steps:
                    r = source(step, d, k)
                    for far in passed_on(step, d, k):
                        to_y(step, d, h, k, far, r)
                    if d == 0 and k > 2:
                        for o in (1, 3):
                            to_z(o, h, r, y_recv.at[k - 1, ZN - o, h])
                    to_sibling(step, d, h, k, r)

    from_y(1, 0)
    from_y(2, 0)
    from_z(1)
    from_z(3)

    arrived(ra.at[pl.ds(0, YN - 1)], g_recv.at[0])
    part[...] = jnp.sum(ra[...], axis=0)
    rb[w] = part[...]
    for o in range(1, WN):
        send(part, rb.at[w], sent.at[6], g_recv.at[1], at_row(w_row(o)))

    from_y(3, 0)
    from_z(2)
    from_y(1, 1, 3)
    from_y(4, 0)
    from_y(1, 2)
    from_y(2, 2)

    arrived(rb.at[pl.ds(0, WN - 1)], g_recv.at[1])
    final[y] = jnp.sum(rb[...], axis=0)
    for o in range(1, YN):
        send(final.at[y], final.at[y], sent.at[7], g_recv.at[2], at_row(y_row(o)))

    from_y(2, 1, 3)
    from_y(3, 1, 3)
    from_y(4, 1, 3)
    from_y(3, 2)
    from_y(4, 2)

    arrived(final.at[pl.ds(0, YN - 1)], g_recv.at[2])
    for q in range(YN):
        wg_out[(q // 2) * 8:(q // 2) * 8 + 8, (q % 2) * TILE:(q % 2 + 1) * TILE] = final[q]

    arrived(x.at[pl.ds(0, BLOCKS * ROWS // CORES)], s_recv.at[0])

    for load in loads[4:]:
        load.wait()
    in_use = count[0]
    first = row * BLOCKS
    group = 11
    total = jnp.zeros((BLOCKS * FEAT, TILE), jnp.float32)
    for g in range(0, SLOTS, group):
        pieces = []
        for t in range(g, g + group):
            here = x[coords[0, t]]
            j = jnp.where(t < in_use, coords[1, t] - first, -1)
            zero = jnp.zeros_like(here)
            pieces.append(jnp.concatenate(
                [jnp.where(j == b, here, zero) for b in range(BLOCKS)], axis=0))
        total += jnp.dot(
            jnp.concatenate(pieces, axis=1),
            tiles[g:g + group].reshape(group * TILE, TILE),
            preferred_element_type=jnp.float32,
        )
    for b in range(BLOCKS):
        fg_out[:, b * TILE:(b + 1) * TILE] = total[b * FEAT:(b + 1) * FEAT].astype(jnp.bfloat16)

    for n, ref in enumerate((
        wpart.at[pl.ds(0, others)], masked.at[pl.ds(0, PARTS * others)],
        x.at[pl.ds(0, len(z_sends) * PART)], x.at[pl.ds(0, len(y_sends) * PART)],
        x.at[pl.ds(0, BLOCKS * ROWS // CORES)],
        wl.at[pl.ds(0, YN - 1)], rb.at[pl.ds(0, WN - 1)], final.at[pl.ds(0, YN - 1)],
    )):
        arrived(ref, sent.at[n])


def shards(grad_out, pre_act, aggregated, weight, tiles, tile_coords, tile_count):
    bf16, f32 = jnp.bfloat16, jnp.float32
    vmem, dma = pltpu.VMEM, pltpu.SemaphoreType.DMA
    return pl.pallas_call(
        kernel,
        out_shape=(
            vmem((FEAT, NODES), bf16),
            vmem((FEAT, COLS * FEAT), f32),
        ),
        in_specs=[pl.BlockSpec(memory_space=pl.ANY)] * 7,
        out_specs=(pl.BlockSpec(memory_space=vmem), pl.BlockSpec(memory_space=vmem)),
        scratch_shapes=[
            vmem((FEAT, NODES), bf16),
            vmem((FEAT, NODES), bf16),
            vmem((FEAT, NODES), bf16),
            vmem((FEAT, COLS * FEAT), bf16),
            vmem((SLOTS, TILE, TILE), bf16),
            pltpu.SMEM((2, SLOTS), jnp.int32),
            pltpu.SMEM((1,), jnp.int32),
            vmem((PARTS * COLS, FEAT, PNODES), bf16),
            vmem((COLS, FEAT, TILE), bf16),
            vmem((TILE, COLS * FEAT), f32),
            vmem((ROWS * BLOCKS, FEAT, TILE), bf16),
            vmem((YN, 8, TILE), f32),
            vmem((YN, 8, TILE), f32),
            vmem((8, TILE), f32),
            vmem((WN, 8, TILE), f32),
            vmem((YN, 8, TILE), f32),
            dma((7,)),
            dma((8,)), dma((1,)), dma((PARTS,)), dma((ZN, PARTS)), dma((YN // 2, ZN, PARTS)), dma((1,)), dma((3,)),
        ],
        compiler_params=pltpu.CompilerParams(
            collective_id=0, has_side_effects=True, vmem_limit_bytes=55168 * 1024,
        ),
        cost_estimate=pl.CostEstimate(flops=300_000_000, bytes_accessed=6_000_000, transcendentals=0),
    )(grad_out, pre_act, aggregated, weight.T, tiles, tile_coords.T, tile_count)


def solution(mesh):
    in_specs = (
        P("col", "row"),
        P("col", "row"),
        P("col", "row"),
        P(None, "col"),
        P("row", None, None),
        P("row", None),
        P("row"),
    )
    out_specs = (P("col", "row"), P("col", None))
    return jax.shard_map(shards, mesh=mesh, in_specs=in_specs, out_specs=out_specs, check_vma=False)
```
